32 devices in a mesh: wave: 8 (over y, x, core), freq: 4 (over z).
Axes of the slice: x: 2, y: 2, z: 4, core: 2. Of those that a mesh axis runs over, the one named last changes fastest.
Arguments:
- res_re: float32 [2048, 8192], P('wave', 'freq'), may hold values from -6 to 6
- res_im: float32 [2048, 8192], P('wave', 'freq'), may hold values from -6 to 6
- basis_re: float32 [256, 8192], P(None, 'freq'), may hold values from -0.046875 to 0.046875
- basis_im: float32 [256, 8192], P(None, 'freq'), may hold values from -0.046875 to 0.046875
- lengths: int32 [2048], P('wave'), may hold values from 8 to 64
- pivots: int32 [128], replicated, may hold values from 0 to 2047, as said below
Outputs:
- coef_re: float32 [2048, 128], P('wave')
- coef_im: float32 [2048, 128], P('wave')
- new_re: float32 [2048, 8192], P('wave', 'freq')
- new_im: float32 [2048, 8192], P('wave', 'freq')
- errors: float32 [2048], P('wave')
The draws below stay inside these ranges and needn't reach their ends.
Inputs may be any that keep to these rules, and one draw needn't show every extreme that they name: The 128 pivots are distinct waveform indices.
All inputs are finite; a program needn't handle non-finite values. Where the reference program divides by a largest or mean magnitude, that divisor is 1e-20 or more.
Results may differ from the reference program's by a relative error of at most 0.0003.
Values sent between devices are 32-bit elements; how exact they have to be, the bound alone decides.
No kernel may reach another device: no remote copies, remote signals or barrier semaphores. Data moves between devices by JAX's collectives and lax.ppermute only.
A program may use at most 64 MiB of HBM per device.

```python
import jax
import jax.numpy as jnp
from jax import lax

NF = 8192
BIN_BLOCK = 128
NB = 256
NP = 128
NS_STEPS = 6
WAVES = 2048


def draw_pivots(key, part):
    chosen = jax.random.permutation(jax.random.fold_in(key, 7), WAVES)
    return chosen[:NP].astype(jnp.int32)


def touch_ends(result, stream_key, least, high):
    longest = result.shape.index(max(result.shape))
    spots = []
    for shift in (0, 1):
        where = [jax.random.randint(jax.random.fold_in(stream_key, axis), (), 0, length) for axis, length in enumerate(result.shape)]
        where[longest] = (where[longest] + shift) % result.shape[longest]
        spots.append(tuple(where))
    return result.at[spots[0]].set(least).at[spots[1]].set(high)


def shard_levels(rng, extent, split, least, high):
    loudness, own = 1.0, jax.random.fold_in(rng, 6)
    for position, blocks in split:
        draws = jnp.exp(jax.random.uniform(jax.random.fold_in(own, position), (blocks,), jnp.float32, least / len(split), high / len(split)))
        loudness = loudness * jnp.repeat(draws, extent[position] // blocks).reshape([-1 if axis == position else 1 for axis in range(len(extent))])
    return loudness


def normal_values(stream_key, shape, spread, most, cuts=(), kind=jnp.bfloat16):
    drawn = spread * jax.random.normal(stream_key, shape, jnp.float32)
    if cuts:
        drawn = drawn * shard_levels(stream_key, shape, cuts, -0.22, 0.18)
    return jnp.clip(drawn, -most, most).astype(kind)


def setup_inputs(seed: int = 0) -> dict:
    arg_keys = jax.random.split(jax.random.key(seed), 7)
    return {
        "res_re": normal_values(arg_keys[0], (WAVES, NF), 1.0, 6.0, ((0, 8), (1, 4)), jnp.float32),
        "res_im": normal_values(arg_keys[1], (WAVES, NF), 1.0, 6.0, ((0, 8), (1, 4)), jnp.float32),
        "basis_re": normal_values(arg_keys[2], (NB, NF), (2 * NF) ** -0.5, 0.046875, ((1, 4),), jnp.float32),
        "basis_im": normal_values(arg_keys[3], (NB, NF), (2 * NF) ** -0.5, 0.046875, ((1, 4),), jnp.float32),
        "lengths": touch_ends(jax.random.randint(arg_keys[4], (WAVES,), NF // BIN_BLOCK // 8, NF // BIN_BLOCK + 1), jax.random.fold_in(arg_keys[4], 1), NF // BIN_BLOCK // 8, (NF // BIN_BLOCK + 1) - 1).astype(jnp.int32),
        "pivots": draw_pivots(jax.random.fold_in(arg_keys[6], 71), 0),
    }


epsilon = 1e-06

def plain(left, right):
    return jnp.dot(left, right, precision=lax.Precision.HIGHEST, preferred_element_type=jnp.float32)

def against(left, right):
    return lax.dot_general(left, right, (((1,), (1,)), ((), ())), precision=lax.Precision.HIGHEST, preferred_element_type=jnp.float32)

def product(left_re, left_im, right_re, right_im):
    return (plain(left_re, right_re) - plain(left_im, right_im), plain(left_re, right_im) + plain(left_im, right_re))

def inner(left_re, left_im, right_re, right_im):
    return (against(left_re, right_re) + against(left_im, right_im), against(left_im, right_re) - against(left_re, right_im))

def whiten(gram_re, gram_im, pivot_re, pivot_im):
    scale = 1.0 / jnp.sqrt(jnp.diagonal(gram_re) + epsilon)
    outer = scale[:, None] * scale[None, :]
    gram_re = gram_re * outer
    gram_im = gram_im * outer
    unit_re = pivot_re * scale[:, None]
    unit_im = pivot_im * scale[:, None]
    bound = jnp.max(lax.optimization_barrier(jnp.sum(jnp.abs(gram_re) + jnp.abs(gram_im), axis=1)))
    ident = jnp.eye(gram_re.shape[0], dtype=jnp.float32)
    your_re = gram_re / bound
    your_im = gram_im / bound
    zed_re = ident
    zed_im = jnp.zeros_like(ident)
    for step in range(NS_STEPS):
        mix_re, mix_im = product(zed_re, zed_im, your_re, your_im)
        step_re = 1.5 * ident - 0.5 * mix_re
        step_im = -0.5 * mix_im
        your_re, your_im = product(your_re, your_im, step_re, step_im)
        zed_re, zed_im = product(step_re, step_im, zed_re, zed_im)
    factor = 1.0 / jnp.sqrt(bound)
    return product(zed_re * factor, zed_im * factor, unit_re, unit_im)

def reference(res_re, res_im, basis_re, basis_im, lengths, pivots):
    bins = jnp.arange(NF, dtype=jnp.int32)
    mask = (bins[None, :] < BIN_BLOCK * lengths[:, None]).astype(jnp.float32)
    live_re = res_re * mask
    live_im = res_im * mask
    pivot_re = live_re[pivots]
    pivot_im = live_im[pivots]
    for sweep in range(2):
        proj_re, proj_im = inner(pivot_re, pivot_im, basis_re, basis_im)
        back_re, back_im = product(proj_re, proj_im, basis_re, basis_im)
        pivot_re = pivot_re - back_re
        pivot_im = pivot_im - back_im
    gram_re, gram_im = inner(pivot_re, pivot_im, pivot_re, pivot_im)
    block_re, block_im = whiten(gram_re, gram_im, pivot_re, pivot_im)
    coef_re, coef_im = inner(live_re, live_im, block_re, block_im)
    back_re, back_im = product(coef_re, coef_im, block_re, block_im)
    new_re = (live_re - back_re) * mask
    new_im = (live_im - back_im) * mask
    errors = lax.optimization_barrier(jnp.sum(new_re * new_re + new_im * new_im, axis=1)) / (BIN_BLOCK * lengths).astype(jnp.float32)
    return (coef_re, coef_im, new_re, new_im, errors)
```

```python
import functools
import math

import jax
import jax.numpy as jnp
from jax import lax
from jax.experimental import pallas as pl
from jax.experimental.pallas import tpu as pltpu
from jax.sharding import PartitionSpec as P

BIN_BLOCK = 128
NS_STEPS = 6
epsilon = 1e-06
F32 = jnp.float32
BF16 = jnp.bfloat16
VMEM_LIMIT = 56 * 1024 * 1024

ANY = pl.BlockSpec(memory_space=pl.ANY)
SMEM = pl.BlockSpec(memory_space=pltpu.SMEM)
VMEM = pl.BlockSpec(memory_space=pltpu.VMEM)


def params():
    return pltpu.CompilerParams(vmem_limit_bytes=VMEM_LIMIT)


def up(value, step):
    return -(-value // step) * step


def swap(array, axis, size, distance):
    return lax.ppermute(array, axis, [(i, i ^ distance) for i in range(size)])


def split(value):
    high = value.astype(BF16)
    low = (value - high.astype(F32)).astype(BF16)
    return high, low


def split3(value):
    high = value.astype(BF16)
    rest = value - high.astype(F32)
    middle = rest.astype(BF16)
    low = (rest - middle.astype(F32)).astype(BF16)
    return high, middle, low


def nn(left, right):
    return jnp.dot(left, right, preferred_element_type=F32)


def nt(left, right):
    return lax.dot_general(left, right, (((1,), (1,)), ((), ())), preferred_element_type=F32)


def nn3(left, right):
    return nn(left[0], right[0]) + (nn(left[0], right[1]) + nn(left[1], right[0]))


def nt3(left, right):
    return nt(left[0], right[0]) + (nt(left[0], right[1]) + nt(left[1], right[0]))


def pick_kernel(cap, piv, lens, meta, re, im, out, where, rows_re, rows_im, sem):
    wave_rows, cols = re.shape
    base = meta[0] * wave_rows
    first_bin = meta[1] * cols
    skip = meta[2]

    def clear(slot, carry):
        where[slot] = -1
        return carry

    lax.fori_loop(0, rows_re.shape[0], clear, 0)

    def look(i, seen):
        row = piv[i] - base
        own = (row >= 0) & (row < wave_rows)
        slot = seen - skip

        @pl.when(own & (slot >= 0) & (slot < cap))
        def _():
            where[slot] = row

        return seen + own.astype(jnp.int32)

    lax.fori_loop(0, piv.shape[0], look, 0)

    def copies(slot):
        row = jnp.maximum(where[slot], 0)
        return (
            pltpu.make_async_copy(re.at[pl.ds(row, 1)], rows_re.at[pl.ds(slot, 1)], sem.at[0]),
            pltpu.make_async_copy(im.at[pl.ds(row, 1)], rows_im.at[pl.ds(slot, 1)], sem.at[1]),
        )

    def start(slot, carry):
        for copy in copies(slot):
            copy.start()
        return carry

    slots = rows_re.shape[0]
    lax.fori_loop(0, slots, start, 0)
    pltpu.make_async_copy(re.at[pl.ds(0, slots)], rows_re, sem.at[0]).wait()
    pltpu.make_async_copy(im.at[pl.ds(0, slots)], rows_im, sem.at[1]).wait()
    bins = lax.broadcasted_iota(jnp.int32, (1, cols), 1) + first_bin

    for slot in range(cap):
        row = where[slot]
        live = jnp.where(row >= 0, lens[jnp.maximum(row, 0)], 0) * BIN_BLOCK
        keep = bins < live
        out[slot : slot + 1, :] = jnp.where(keep, rows_re[slot : slot + 1, :], 0.0)
        out[cap + slot : cap + slot + 1, :] = jnp.where(keep, rows_im[slot : slot + 1, :], 0.0)


def pick(cap, pivots, lengths, meta, res_re, res_im):
    cols = res_re.shape[1]
    return pl.pallas_call(
        functools.partial(pick_kernel, cap),
        out_shape=jax.ShapeDtypeStruct((2 * cap, cols), F32),
        in_specs=[SMEM, SMEM, SMEM, ANY, ANY],
        out_specs=VMEM,
        scratch_shapes=[
            pltpu.SMEM((up(cap, 8),), jnp.int32),
            pltpu.VMEM((up(cap, 8), cols), F32),
            pltpu.VMEM((up(cap, 8), cols), F32),
            pltpu.SemaphoreType.DMA((2,)),
        ],
        compiler_params=params(),
        name="pick",
    )(pivots, lengths, meta, res_re, res_im)


def cross_kernel(cap, meta, rows, b_re, b_im, out):
    nb, cols = b_re.shape
    mine = out.shape[0] - up(cap, 8)
    start = pl.multiple_of(meta[0] * mine, mine)
    chunk = min(cols, 512)
    total = jnp.zeros((2 * cap + 2 * mine, 2 * nb), F32)
    for at in range(0, cols, chunk):
        part = pl.ds(at, chunk)
        left = split(
            jnp.concatenate([rows[:, part], b_re[pl.ds(start, mine), part], b_im[pl.ds(start, mine), part]], axis=0)
        )
        right = split(jnp.concatenate([b_re[:, part], b_im[:, part]], axis=0))
        total += nt3(left, right)

    def join(at, size):
        real, imag = total[at : at + size], total[at + size : at + 2 * size]
        return jnp.concatenate([real[:, :nb] + imag[:, nb:], imag[:, :nb] - real[:, nb:]], axis=1)

    out[...] = jnp.zeros_like(out)
    out[0:cap, :] = join(0, cap)
    out[up(cap, 8) :, :] = join(2 * cap, mine)


def cross(cap, mine, meta, rows, basis_re, basis_im):
    nb = basis_re.shape[0]
    return pl.pallas_call(
        functools.partial(cross_kernel, cap),
        out_shape=jax.ShapeDtypeStruct((up(cap, 8) + mine, 2 * nb), F32),
        in_specs=[SMEM, VMEM, VMEM, VMEM],
        out_specs=VMEM,
        compiler_params=params(),
        name="cross",
    )(meta, rows, basis_re, basis_im)


def parts_kernel(re, im, lens, meta, high, low):
    cols = re.shape[1]
    rows = re.shape[0]
    bins = lax.broadcasted_iota(jnp.int32, (1, cols), 1) + meta[1] * cols
    keep = bins < lens[...] * BIN_BLOCK
    for at, ref in ((0, re), (rows, im)):
        high_part, low_part = split(jnp.where(keep, ref[...], 0.0))
        high[at : at + rows, :] = high_part
        low[at : at + rows, :] = low_part


def parts(res_re, res_im, lens, meta):
    rows, cols = res_re.shape
    shape = jax.ShapeDtypeStruct((2 * rows, cols), BF16)
    return pl.pallas_call(
        parts_kernel,
        out_shape=(shape, shape),
        in_specs=[VMEM, VMEM, VMEM, SMEM],
        out_specs=(VMEM, VMEM),
        compiler_params=params(),
        name="parts",
    )(res_re, res_im, lens, meta)


def ranks(pivots_col, pivots_row, wave_rows):
    count = pivots_col.shape[0]
    owner_col = pivots_col // wave_rows
    owner_row = pivots_row // wave_rows
    i = lax.broadcasted_iota(jnp.int32, (count, count), 0)
    j = lax.broadcasted_iota(jnp.int32, (count, count), 1)
    ahead = (owner_col == owner_row) & (j < i)
    return owner_col, jnp.sum(ahead.astype(jnp.int32), axis=1, keepdims=True)


def one_hot(index, width):
    return (lax.broadcasted_iota(jnp.int32, (index.shape[0], width), 1) == index).astype(F32).astype(BF16)


def project_kernel(cap, nw, nf, places, n_cross, meta, pc, pr, extra_p, extra_c, b_re, b_im, r_high, r_low, *refs):
    list_refs, refs = refs[: len(places)], refs[len(places) :]
    cross_refs, refs = refs[:n_cross], refs[n_cross:]
    p_out, g_out, refs = refs[0], refs[1], refs[2:]
    d_out, refs = refs[:nf], refs[nf:]
    gathered, crossed, gram_b, basis, left_high, left_low, more_p, more_c, d_all, sem_l, sem_c, sem_b, sem_x = refs
    count = pc.shape[0]
    nb, cols = b_re.shape
    waves = r_high.shape[0] // 2
    capp = up(cap, 8)
    mine = nb // nw
    me_w, me_f, over = meta[0], meta[1], meta[3]

    def move(source, target, sem):
        copy = pltpu.make_async_copy(source, target, sem)
        copy.start()
        return copy

    waits = []
    for k, ref in enumerate(cross_refs):
        waits.append(move(ref.at[pl.ds(0, capp)], crossed.at[pl.ds(k * capp, capp)], sem_c.at[2 * k]))
        place = pl.multiple_of((me_w ^ k) * mine, mine)
        waits.append(move(ref.at[pl.ds(capp, mine)], gram_b.at[pl.ds(place, mine)], sem_c.at[2 * k + 1]))
    list_waits = []
    for index, ((k, col), ref) in enumerate(zip(places, list_refs)):
        target = gathered.at[pl.ds(k * 2 * cap, 2 * cap), pl.ds(col, ref.shape[1])]
        list_waits.append(move(ref, target, sem_l.at[index]))
    basis_waits = [
        move(b_re, basis.at[pl.ds(0, nb)], sem_b.at[0]),
        move(b_im, basis.at[pl.ds(nb, nb)], sem_b.at[1]),
    ]
    left_waits = [
        move(r_high, left_high, sem_b.at[2]),
        move(r_low, left_low, sem_b.at[3]),
    ]

    @pl.when(over > 0)
    def _():
        first = pltpu.make_async_copy(extra_p, more_p, sem_x.at[0])
        second = pltpu.make_async_copy(extra_c, more_c, sem_x.at[1])
        first.start()
        second.start()
        first.wait()
        second.wait()

    owner, rank = ranks(pc[...], pr[...], waves)
    held = rank < cap
    group = jnp.bitwise_xor(owner, me_w)
    nowhere = jnp.full_like(rank, -1)
    at_re = jnp.where(held, group * (2 * cap) + rank, nowhere)
    at_im = jnp.where(held, group * (2 * cap) + cap + rank, nowhere)
    at_c = jnp.where(held, group * capp + rank, nowhere)
    select = one_hot(jnp.concatenate([at_re, at_im], axis=0), nw * 2 * cap)
    select_c = one_hot(at_c, nw * capp)

    for copy in waits:
        copy.wait()
    pieces = split3(crossed[...])
    cross_all = nn(select_c, pieces[0]) + (nn(select_c, pieces[1]) + nn(select_c, pieces[2]))
    cross_all = cross_all + jnp.where(over > 0, more_c[...], 0.0)
    stacked = jnp.concatenate([cross_all[:, :nb], cross_all[:, nb:]], axis=0)
    twist = nn3(split(stacked), split(gram_b[...]))
    total_re = 2.0 * cross_all[:, :nb] - (twist[:count, :nb] - twist[count:, nb:])
    total_im = 2.0 * cross_all[:, nb:] - (twist[:count, nb:] + twist[count:, :nb])
    take = split(
        jnp.concatenate(
            [jnp.concatenate([total_re, -total_im], axis=1), jnp.concatenate([total_im, total_re], axis=1)], axis=0
        )
    )

    for copy in list_waits:
        copy.wait()
    for copy in basis_waits:
        copy.wait()
    for copy in left_waits:
        copy.wait()
    chunk = min(cols, 512)
    inner_r = jnp.zeros((2 * waves, 2 * count), F32)
    inner_p = jnp.zeros((2 * count, 2 * count), F32)
    for begin in range(0, cols, chunk):
        part = pl.ds(begin, chunk)
        high, low = split(gathered[:, part])
        block = nn(select, high) + nn(select, low)
        block = block + jnp.where(over > 0, more_p[:, part], 0.0)
        block = block - nn3(take, split(basis[:, part]))
        p_out[:, part] = block
        right = split(block)
        inner_p += nt3(right, right)
        inner_r += nt3((left_high[:, part], left_low[:, part]), right)

    gram_re = inner_p[:count, :count] + inner_p[count:, count:]
    gram_im = inner_p[count:, :count] - inner_p[:count, count:]
    i = lax.broadcasted_iota(jnp.int32, (count, count), 0)
    j = lax.broadcasted_iota(jnp.int32, (count, count), 1)
    g_out[...] = jnp.where(i <= j, gram_re, gram_im)
    d_all[:, :count] = inner_r[:waves, :count] + inner_r[waves:, count:]
    d_all[:, count:] = inner_r[waves:, :count] - inner_r[:waves, count:]
    share = waves // nf
    for k in range(nf):
        d_out[k][...] = d_all[pl.ds(pl.multiple_of((me_f ^ k) * share, share), share), :]


def project(cap, nw, nf, places, meta, pivots, extra_p, extra_c, basis_re, basis_im, r_high, r_low, lists, crosses):
    count = pivots.shape[0]
    nb, cols = basis_re.shape
    waves = r_high.shape[0] // 2
    capp = up(cap, 8)
    shapes = [
        jax.ShapeDtypeStruct((2 * count, cols), F32),
        jax.ShapeDtypeStruct((count, count), F32),
    ] + [jax.ShapeDtypeStruct((waves // nf, 2 * count), F32)] * nf
    return pl.pallas_call(
        functools.partial(project_kernel, cap, nw, nf, places, len(crosses)),
        out_shape=shapes,
        in_specs=[SMEM, VMEM, VMEM] + [ANY] * (6 + len(lists) + len(crosses)),
        out_specs=[VMEM] * len(shapes),
        scratch_shapes=[
            pltpu.VMEM((nw * 2 * cap, cols), F32),
            pltpu.VMEM((nw * capp, 2 * nb), F32),
            pltpu.VMEM((nb, 2 * nb), F32),
            pltpu.VMEM((2 * nb, cols), F32),
            pltpu.VMEM((2 * waves, cols), BF16),
            pltpu.VMEM((2 * waves, cols), BF16),
            pltpu.VMEM((2 * count, cols), F32),
            pltpu.VMEM((count, 2 * nb), F32),
            pltpu.VMEM((waves, 2 * count), F32),
            pltpu.SemaphoreType.DMA((len(lists),)),
            pltpu.SemaphoreType.DMA((2 * len(crosses),)),
            pltpu.SemaphoreType.DMA((4,)),
            pltpu.SemaphoreType.DMA((2,)),
        ],
        compiler_params=params(),
        name="project",
    )(
        meta,
        pivots.reshape(count, 1),
        pivots.reshape(1, count),
        extra_p,
        extra_c,
        basis_re,
        basis_im,
        r_high,
        r_low,
        *lists,
        *crosses,
    )


def whiten_kernel(nf, *refs):
    packed = refs[0][...]
    for ref in refs[1:nf]:
        packed = packed + ref[...]
    out = refs[nf]
    count = packed.shape[0]
    i = lax.broadcasted_iota(jnp.int32, (count, count), 0)
    j = lax.broadcasted_iota(jnp.int32, (count, count), 1)
    upper = jnp.where(i <= j, packed, 0.0)
    lower = jnp.where(i > j, packed, 0.0)
    diagonal = jnp.where(i == j, packed, 0.0)
    gram_re = upper + upper.T - diagonal
    gram_im = lower - lower.T
    scale_row = 1.0 / jnp.sqrt(jnp.sum(diagonal, axis=0, keepdims=True) + epsilon)
    scale_col = 1.0 / jnp.sqrt(jnp.sum(diagonal, axis=1, keepdims=True) + epsilon)
    outer = scale_col * scale_row
    gram_re = gram_re * outer
    gram_im = gram_im * outer
    bound = jnp.max(jnp.sum(jnp.abs(gram_re) + jnp.abs(gram_im), axis=1, keepdims=True), axis=0, keepdims=True)
    gram_re = gram_re / bound
    gram_im = gram_im / bound
    mix = jnp.concatenate(
        [jnp.concatenate([gram_re, gram_im], axis=1), jnp.concatenate([-gram_im, gram_re], axis=1)], axis=0
    )
    i = lax.broadcasted_iota(jnp.int32, (2 * count, 2 * count), 0)
    j = lax.broadcasted_iota(jnp.int32, (2 * count, 2 * count), 1)
    ident = jnp.where(i == j, 1.0, 0.0).astype(F32)
    zed = None
    for step in range(NS_STEPS):
        turn = 1.5 * ident - 0.5 * mix
        turn_parts = split(turn)
        zed = turn if zed is None else nn3(turn_parts, split(zed))
        if step < NS_STEPS - 1:
            mix = nn3(split(nn3(split(mix), turn_parts)), turn_parts)
    out[...] = zed * (1.0 / jnp.sqrt(bound)) * jnp.concatenate([scale_row, scale_row], axis=1)


def whiten(grams):
    count = grams[0].shape[0]
    return pl.pallas_call(
        functools.partial(whiten_kernel, len(grams)),
        out_shape=jax.ShapeDtypeStruct((2 * count, 2 * count), F32),
        in_specs=[VMEM] * len(grams),
        out_specs=VMEM,
        compiler_params=params(),
        name="whiten",
    )(*grams)


def update_kernel(nf, meta, lens, whitener, p, re, im, *refs):
    pieces, refs = refs[:nf], refs[nf:]
    coef_re, coef_im, new_re, new_im, squares, d_all, back_high, back_low, sums = refs
    waves, chunk = re.shape
    count = coef_re.shape[1]
    step = pl.program_id(0)
    share = waves // nf

    @pl.when(step == 0)
    def _():
        for k in range(nf):
            place = pl.multiple_of((meta[1] ^ k) * share, share)
            d_all[pl.ds(place, share), :] = pieces[k][...]
        turn = split(whitener[...])
        coef = nt3(split(d_all[...]), turn)
        coef_re[...] = coef[:, :count]
        coef_im[...] = coef[:, count:]
        back = nn3(split(coef), turn)
        back_re, back_im = back[:, :count], back[:, count:]
        high, low = split(
            jnp.concatenate(
                [jnp.concatenate([back_re, -back_im], axis=1), jnp.concatenate([back_im, back_re], axis=1)], axis=0
            )
        )
        back_high[...] = high
        back_low[...] = low
        sums[...] = jnp.zeros_like(sums)

    change = nn3((back_high[...], back_low[...]), split(p[...]))
    first = meta[1] * (chunk * pl.num_programs(0)) + step * chunk
    bins = lax.broadcasted_iota(jnp.int32, (1, chunk), 1) + first
    keep = bins < lens[...] * BIN_BLOCK
    now_re = jnp.where(keep, re[...] - change[:waves], 0.0)
    now_im = jnp.where(keep, im[...] - change[waves:], 0.0)
    new_re[...] = now_re
    new_im[...] = now_im
    square = now_re * now_re + now_im * now_im
    total = square[:, :128]
    for at in range(128, chunk, 128):
        total = total + square[:, at : at + 128]
    sums[...] += total

    @pl.when(step == pl.num_programs(0) - 1)
    def _():
        squares[...] = jnp.sum(sums[...].T, axis=0, keepdims=True)


def update(nf, meta, lens, whitener, p, res_re, res_im, pieces):
    waves, cols = res_re.shape
    count = p.shape[0] // 2
    share = waves // nf
    chunk = min(cols, 512)
    whole = lambda *shape: pl.BlockSpec(shape, lambda s: (0,) * len(shape))
    block = pl.BlockSpec((waves, chunk), lambda s: (0, s))
    return pl.pallas_call(
        functools.partial(update_kernel, nf),
        grid=(cols // chunk,),
        out_shape=[
            jax.ShapeDtypeStruct((waves, count), F32),
            jax.ShapeDtypeStruct((waves, count), F32),
            jax.ShapeDtypeStruct((waves, cols), F32),
            jax.ShapeDtypeStruct((waves, cols), F32),
            jax.ShapeDtypeStruct((1, waves), F32),
        ],
        in_specs=[
            SMEM,
            whole(waves, 1),
            whole(2 * count, 2 * count),
            pl.BlockSpec((2 * count, chunk), lambda s: (0, s)),
            block,
            block,
        ]
        + [whole(share, 2 * count)] * nf,
        out_specs=[whole(waves, count), whole(waves, count), block, block, whole(1, waves)],
        scratch_shapes=[
            pltpu.VMEM((waves, 2 * count), F32),
            pltpu.VMEM((2 * waves, 2 * count), BF16),
            pltpu.VMEM((2 * waves, 2 * count), BF16),
            pltpu.VMEM((waves, 128), F32),
        ],
        compiler_params=params(),
        name="update",
    )(meta, lens, whitener, p, res_re, res_im, *pieces)


def spread(rows, nw):
    half = rows.shape[1] // 2
    found = [(0, 0, rows)]
    if nw == 8:
        by_two = swap(rows, "wave", nw, 2)
        by_four = swap(rows, "wave", nw, 4)
        found.append((2, 0, by_two))
        found.append((4, 0, by_four))
        found.append((6, 0, swap(by_two[:, :half], "wave", nw, 4)))
        found.append((6, half, swap(by_four[:, half:], "wave", nw, 2)))
    else:
        found += [(k, 0, swap(rows, "wave", nw, k)) for k in range(2, nw, 2)]
    return found + [(k + 1, col, swap(array, "wave", nw, 1)) for k, col, array in found]


def spread_small(rows, nw):
    found = [rows] + [swap(rows, "wave", nw, k) for k in range(2, nw, 2)]
    both = []
    for array in found:
        both += [array, swap(array, "wave", nw, 1)]
    return both


def sum_over_freq(array, nf):
    return sum([swap(array, "freq", nf, k) for k in range(1, nf)], array)


def capacity(count, nw, rows):
    mean = count / nw
    return min(up(math.ceil(mean + 3.0 * math.sqrt(mean)), 4), count, rows)


def body(nw, nf, res_re, res_im, basis_re, basis_im, lengths, pivots):
    waves, cols = res_re.shape
    nb = basis_re.shape[0]
    count = pivots.shape[0]
    cap = capacity(count, nw, waves)
    capp = up(cap, 8)
    mine = nb // nw
    me_w = lax.axis_index("wave").astype(jnp.int32)
    me_f = lax.axis_index("freq").astype(jnp.int32)
    zero = jnp.zeros((), jnp.int32)
    lens = lengths.reshape(waves, 1)
    owners = pivots // waves
    counts = jnp.sum((owners[:, None] == jnp.arange(nw, dtype=jnp.int32)[None, :]).astype(jnp.int32), axis=0)
    rounds = (jnp.max(counts) + cap - 1) // cap

    rows = pick(cap, pivots, lengths, jnp.stack([me_w, me_f, zero, zero]), res_re, res_im)
    found = spread(rows, nw)
    meta = jnp.stack([me_w, me_f, zero, (rounds > 1).astype(jnp.int32)])
    partial = cross(cap, mine, meta, rows, basis_re, basis_im)
    crosses = spread_small(sum_over_freq(partial, nf), nw)
    r_high, r_low = parts(res_re, res_im, lens, meta)

    def another(carry):
        turn, extra_p, extra_c = carry
        more = pick(cap, pivots, lengths, jnp.stack([me_w, me_f, turn * cap, zero]), res_re, res_im)
        more_c = lax.psum(cross(cap, mine, meta, more, basis_re, basis_im)[:cap], "freq")
        all_p = lax.all_gather(more, "wave")
        all_c = lax.all_gather(more_c, "wave")
        rank = jnp.sum(
            ((owners[:, None] == owners[None, :]) & (jnp.arange(count)[None, :] < jnp.arange(count)[:, None])).astype(
                jnp.int32
            ),
            axis=1,
        ) - turn * cap
        slot = jnp.where((rank >= 0) & (rank < cap), owners * cap + rank, -1)
        chosen = (slot[:, None] == jnp.arange(nw * cap)[None, :]).astype(F32)
        place = lambda table: jnp.dot(chosen, table, precision=lax.Precision.HIGHEST, preferred_element_type=F32)
        added = jnp.concatenate(
            [place(all_p[:, :cap].reshape(nw * cap, cols)), place(all_p[:, cap:].reshape(nw * cap, cols))], axis=0
        )
        return turn + 1, extra_p + added, extra_c + place(all_c.reshape(nw * cap, 2 * nb))

    _, extra_p, extra_c = lax.while_loop(
        lambda carry: carry[0] < rounds,
        another,
        (jnp.ones((), jnp.int32), jnp.zeros((2 * count, cols), F32), jnp.zeros((count, 2 * nb), F32)),
    )

    places = tuple((k, col) for k, col, _ in found)
    p, gram, *pieces = project(
        cap,
        nw,
        nf,
        places,
        meta,
        pivots,
        extra_p,
        extra_c,
        basis_re,
        basis_im,
        r_high,
        r_low,
        [array for _, _, array in found],
        crosses,
    )
    piece = sum([swap(pieces[k], "freq", nf, k) for k in range(1, nf)], pieces[0])
    grams = [gram] + [swap(gram, "freq", nf, k) for k in range(1, nf)]
    every = [piece] + [swap(piece, "freq", nf, k) for k in range(1, nf)]
    whitener = whiten(grams)
    coef_re, coef_im, new_re, new_im, squares = update(nf, meta, lens, whitener, p, res_re, res_im, every)
    errors = sum_over_freq(squares, nf).reshape(waves) / (BIN_BLOCK * lengths).astype(F32)
    return coef_re, coef_im, new_re, new_im, errors


def solution(mesh):
    nw, nf = mesh.shape["wave"], mesh.shape["freq"]
    return jax.shard_map(
        functools.partial(body, nw, nf),
        mesh=mesh,
        in_specs=(P("wave", "freq"), P("wave", "freq"), P(None, "freq"), P(None, "freq"), P("wave"), P()),
        out_specs=(P("wave", None), P("wave", None), P("wave", "freq"), P("wave", "freq"), P("wave")),
        check_vma=False,
    )
```

```python
import functools
import math

import jax
import jax.numpy as jnp
from jax import lax
from jax.experimental import pallas as pl
from jax.experimental.pallas import tpu as pltpu
from jax.sharding import PartitionSpec as P

BIN_BLOCK = 128
NS_STEPS = 6
epsilon = 1e-06
F32 = jnp.float32
BF16 = jnp.bfloat16
MIB = 1024 * 1024

ANY = pl.BlockSpec(memory_space=pl.ANY)
SMEM = pl.BlockSpec(memory_space=pltpu.SMEM)
VMEM = pl.BlockSpec(memory_space=pltpu.VMEM)
HBM = pl.BlockSpec(memory_space=pltpu.HBM)


def params(mib):
    return pltpu.CompilerParams(vmem_limit_bytes=mib * MIB)


def light():
    return pl.CostEstimate(flops=1000, bytes_accessed=1000, transcendentals=0)


def column(row):
    wide = jnp.broadcast_to(row.astype(F32), (8, row.shape[1]))
    return wide.T[:, 0:1].astype(jnp.int32)


def up(value, step):
    return -(-value // step) * step


def swap(array, axis, size, distance):
    return lax.ppermute(array, axis, [(i, i ^ distance) for i in range(size)])


def split(value):
    high = value.astype(BF16)
    low = (value - high.astype(F32)).astype(BF16)
    return high, low


def split3(value):
    high = value.astype(BF16)
    rest = value - high.astype(F32)
    middle = rest.astype(BF16)
    low = (rest - middle.astype(F32)).astype(BF16)
    return high, middle, low


def nn(left, right):
    return jnp.dot(left, right, preferred_element_type=F32)


def nt(left, right):
    return lax.dot_general(left, right, (((1,), (1,)), ((), ())), preferred_element_type=F32)


def nn3(left, right):
    return nn(left[0], right[0]) + (nn(left[0], right[1]) + nn(left[1], right[0]))


def nt3(left, right):
    return nt(left[0], right[0]) + (nt(left[0], right[1]) + nt(left[1], right[0]))


def pick_kernel(cap, piv, lens, skip_ref, re, im, out, where, rows_re, rows_im, sem):
    wave_rows, cols = re.shape
    slots = rows_re.shape[0]
    base = lax.axis_index("wave") * wave_rows
    first_bin = lax.axis_index("freq") * cols
    skip = skip_ref[0]

    def fetch(row, slot):
        pltpu.make_async_copy(re.at[pl.ds(row, 1)], rows_re.at[pl.ds(slot, 1)], sem.at[0]).start()
        pltpu.make_async_copy(im.at[pl.ds(row, 1)], rows_im.at[pl.ds(slot, 1)], sem.at[1]).start()

    def look(i, seen):
        row = piv[i] - base
        own = (row >= 0) & (row < wave_rows)
        slot = seen - skip

        @pl.when(own & (slot >= 0) & (slot < cap))
        def _():
            where[slot] = lens[row]
            fetch(row, slot)

        return seen + own.astype(jnp.int32)

    found = lax.fori_loop(0, piv.shape[0], look, 0, unroll=8) - skip

    def fill(slot, carry):
        where[slot] = 0
        fetch(0, slot)
        return carry

    lax.fori_loop(jnp.clip(found, 0, cap), slots, fill, 0)
    at = lax.broadcasted_iota(jnp.int32, (slots, 1), 0)
    live = jnp.zeros((slots, 1), jnp.int32)
    for slot in range(slots):
        live = jnp.where(at == slot, where[slot] * BIN_BLOCK, live)
    bins = lax.broadcasted_iota(jnp.int32, (slots, cols), 1) + first_bin
    keep = bins < live
    pltpu.make_async_copy(re.at[pl.ds(0, slots)], rows_re, sem.at[0]).wait()
    pltpu.make_async_copy(im.at[pl.ds(0, slots)], rows_im, sem.at[1]).wait()
    out[0:cap, :] = jnp.where(keep, rows_re[...], 0.0)[0:cap]
    out[cap : 2 * cap, :] = jnp.where(keep, rows_im[...], 0.0)[0:cap]


def pick(cap, pivots, lengths, skip, res_re, res_im):
    cols = res_re.shape[1]
    return pl.pallas_call(
        functools.partial(pick_kernel, cap),
        out_shape=jax.ShapeDtypeStruct((2 * cap, cols), F32),
        in_specs=[SMEM, SMEM, SMEM, HBM, HBM],
        out_specs=VMEM,
        scratch_shapes=[
            pltpu.SMEM((up(cap, 8),), jnp.int32),
            pltpu.VMEM((up(cap, 8), cols), F32),
            pltpu.VMEM((up(cap, 8), cols), F32),
            pltpu.SemaphoreType.DMA((2,)),
        ],
        compiler_params=params(8),
        name="pick",
    )(pivots, lengths, skip, res_re, res_im)


def cross_kernel(cap, rows, b_re, b_im, out):
    nb, cols = b_re.shape
    mine = out.shape[0] - up(cap, 8)
    start = pl.multiple_of(lax.axis_index("wave") * mine, mine)
    chunk = min(cols, 512)
    total = jnp.zeros((2 * cap + 2 * mine, 2 * nb), F32)
    for at in range(0, cols, chunk):
        part = pl.ds(at, chunk)
        left = split(
            jnp.concatenate([rows[:, part], b_re[pl.ds(start, mine), part], b_im[pl.ds(start, mine), part]], axis=0)
        )
        right = split(jnp.concatenate([b_re[:, part], b_im[:, part]], axis=0))
        total += nt3(left, right)

    def join(at, size):
        real, imag = total[at : at + size], total[at + size : at + 2 * size]
        return jnp.concatenate([real[:, :nb] + imag[:, nb:], imag[:, :nb] - real[:, nb:]], axis=1)

    out[...] = jnp.zeros_like(out)
    out[0:cap, :] = join(0, cap)
    out[up(cap, 8) :, :] = join(2 * cap, mine)
def cross(cap, nw, rows, basis_re, basis_im):
    nb = basis_re.shape[0]
    return pl.pallas_call(
        functools.partial(cross_kernel, cap),
        out_shape=jax.ShapeDtypeStruct((up(cap, 8) + nb // nw, 2 * nb), F32),
        in_specs=[VMEM, VMEM, VMEM],
        out_specs=VMEM,
        compiler_params=params(16),
        cost_estimate=light(),
        name="cross",
    )(rows, basis_re, basis_im)


def ranks(pivots_col, pivots_row, wave_rows):
    count = pivots_col.shape[0]
    owner_col = pivots_col // wave_rows
    owner_row = pivots_row // wave_rows
    i = lax.broadcasted_iota(jnp.int32, (count, count), 0)
    j = lax.broadcasted_iota(jnp.int32, (count, count), 1)
    ahead = (owner_col == owner_row) & (j < i)
    return owner_col, jnp.sum(ahead.astype(jnp.int32), axis=1, keepdims=True)


def one_hot(index, width):
    return (lax.broadcasted_iota(jnp.int32, (index.shape[0], width), 1) == index).astype(F32).astype(BF16)


def move(source, target, sem):
    copy = pltpu.make_async_copy(source, target, sem)
    copy.start()
    return copy


def orders_kernel(cap, nw, waves, pr, listed, crossed, rounds, blank_p, blank_c):
    owner, rank = ranks(column(pr[...]), pr[...], waves)
    group = jnp.bitwise_xor(owner, lax.axis_index("wave"))
    rounds[0] = jnp.max(rank) // cap + 1
    at = jnp.where(rank < cap, group * (2 * cap) + rank, -nw * 2 * cap)
    both = jnp.concatenate([at, at + cap], axis=0)
    listed[...] = one_hot(both, listed.shape[1])
    capp = crossed.shape[1] // nw
    crossed[...] = one_hot(jnp.where(rank < cap, group * capp + rank, -1), crossed.shape[1])


def orders(cap, nw, waves, nb, cols, pivots):
    count = pivots.shape[0]
    return pl.pallas_call(
        functools.partial(orders_kernel, cap, nw, waves),
        out_shape=(
            jax.ShapeDtypeStruct((2 * count, nw * 2 * cap), BF16),
            jax.ShapeDtypeStruct((count, nw * up(cap, 8)), BF16),
            jax.ShapeDtypeStruct((1,), jnp.int32),
            jax.ShapeDtypeStruct((2 * count, cols), F32),
            jax.ShapeDtypeStruct((count, 2 * nb), F32),
        ),
        in_specs=[VMEM],
        out_specs=(VMEM, VMEM, SMEM, HBM, HBM),
        compiler_params=params(8),
        cost_estimate=light(),
        name="orders",
    )(pivots.reshape(1, count))


def fetch_lists(refs, places, cap, gathered, sem):
    waits = []
    for index, ((k, col), ref) in enumerate(zip(places, refs)):
        target = gathered.at[pl.ds(k * 2 * cap, 2 * cap), pl.ds(col, ref.shape[1])]
        waits.append(move(ref, target, sem.at[index]))
    return waits


def packed(gram_re, gram_im):
    i = lax.broadcasted_iota(jnp.int32, gram_re.shape, 0)
    j = lax.broadcasted_iota(jnp.int32, gram_re.shape, 1)
    return jnp.where(i <= j, gram_re, gram_im)


def joined(total, rows, cols):
    real = total[:rows, :cols] + total[rows:, cols:]
    imag = total[rows:, :cols] - total[:rows, cols:]
    return real, imag


def stack_columns(pair_re, pair_im, target, chunk, sem):
    rows, cols = pair_re.shape
    waits = []
    for step in range(cols // chunk):
        part = pl.ds(step * chunk, chunk)
        waits.append(
            [
                move(pair_re.at[:, part], target.at[pl.ds(0, rows), part], sem.at[step, 0]),
                move(pair_im.at[:, part], target.at[pl.ds(rows, rows), part], sem.at[step, 1]),
            ]
        )
    return waits


def project_kernel(cap, nw, nf, places, rounds, select, select_c, lens, b_re, b_im, re, im, *refs):
    extra_p, extra_c, refs = refs[0], refs[1], refs[2:]
    list_refs, refs = refs[: len(places)], refs[len(places) :]
    cross_refs, refs = refs[:nw], refs[nw:]
    p_out, g_out, refs = refs[0], refs[1], refs[2:]
    out, refs = refs[:nf], refs[nf:]
    gathered, crossed, gram_b, basis, live, placed, more_p, more_c, d_all, sem_l, sem_c, sem_b, sem_x = refs
    count = select_c.shape[0]
    nb, cols = b_re.shape
    waves = re.shape[0]
    capp = up(cap, 8)
    mine = nb // nw
    me_w, me_f, over = lax.axis_index("wave"), lax.axis_index("freq"), rounds[0] > 1
    waits = []
    for k, ref in enumerate(cross_refs):
        at = (k ^ 1) * capp
        waits.append(move(ref.at[pl.ds(0, capp)], crossed.at[pl.ds(at, capp)], sem_c.at[2 * k]))
        at = pl.multiple_of((me_w ^ k) * mine, mine)
        waits.append(move(ref.at[pl.ds(capp, mine)], gram_b.at[pl.ds(at, mine)], sem_c.at[2 * k + 1]))
    list_waits = fetch_lists(list_refs, places, cap, gathered, sem_l)
    chunk = min(cols, 1024)

    @pl.when(over)
    def _():
        first = pltpu.make_async_copy(extra_p, more_p, sem_x.at[0])
        second = pltpu.make_async_copy(extra_c, more_c, sem_x.at[1])
        first.start()
        second.start()
        first.wait()
        second.wait()

    for copy in list_waits:
        copy.wait()
    basis_waits = stack_columns(b_re, b_im, basis, chunk, sem_b)
    for step in range(cols // chunk):
        part = pl.ds(step * chunk, chunk)
        high, low = split(gathered[:, part])
        block = nn(select[...], high) + nn(select[...], low)
        placed[:, part] = block + jnp.where(over, more_p[:, part], 0.0)
    for copy in waits:
        copy.wait()
    pieces = split3(crossed[...])
    cross_all = nn(select_c[...], pieces[0]) + (nn(select_c[...], pieces[1]) + nn(select_c[...], pieces[2]))
    cross_all = cross_all + jnp.where(over, more_c[...], 0.0)
    stacked = jnp.concatenate([cross_all[:, :nb], cross_all[:, nb:]], axis=0)
    twist = nn3(split(stacked), split(gram_b[...]))
    total_re = 2.0 * cross_all[:, :nb] - (twist[:count, :nb] - twist[count:, nb:])
    total_im = 2.0 * cross_all[:, nb:] - (twist[:count, nb:] + twist[count:, :nb])
    take = split(
        jnp.concatenate(
            [jnp.concatenate([total_re, -total_im], axis=1), jnp.concatenate([total_im, total_re], axis=1)], axis=0
        )
    )
    live_waits = [
        move(re, live.at[pl.ds(0, waves)], sem_x.at[2]),
        move(im, live.at[pl.ds(waves, waves)], sem_x.at[3]),
    ]
    for step in range(cols // chunk):
        part = pl.ds(step * chunk, chunk)
        for copy in basis_waits[step]:
            copy.wait()
        placed[:, part] = placed[:, part] - nn3(take, split(basis[:, part]))
    p_wait = move(placed, p_out, sem_x.at[4])
    right = split(placed[...])
    inner_p = nt(right[0], right[0])
    inner_q = nt(right[0], right[1])
    for copy in live_waits:
        copy.wait()
    end = column(lens[...]) * BIN_BLOCK
    keep = lax.broadcasted_iota(jnp.int32, (1, cols), 1) + me_f * cols < end
    inner_re = nt3(split(jnp.where(keep, live[0:waves, :], 0.0)), right)
    inner_im = nt3(split(jnp.where(keep, live[waves : 2 * waves, :], 0.0)), right)
    inner_r = jnp.concatenate([inner_re, inner_im], axis=0)
    g_out[...] = packed(*joined(inner_p + (inner_q + inner_q.T), count, count))
    d_all[:, :count], d_all[:, count:] = joined(inner_r, waves, count)
    share = waves // nf
    for k in range(nf):
        out[k][...] = d_all[pl.ds(pl.multiple_of((me_f ^ k) * share, share), share), :]
    p_wait.wait()


def project(cap, nw, nf, places, rounds, select, select_c, lens, *rest):
    basis_re, res_re = rest[0], rest[2]
    count = select_c.shape[0]
    nb, cols = basis_re.shape
    waves = res_re.shape[0]
    shapes = [jax.ShapeDtypeStruct((2 * count, cols), F32), jax.ShapeDtypeStruct((count, count), F32)]
    shapes += [jax.ShapeDtypeStruct((waves // nf, 2 * count), F32)] * nf
    return pl.pallas_call(
        functools.partial(project_kernel, cap, nw, nf, places),
        out_shape=shapes,
        in_specs=[SMEM] + [VMEM] * 3 + [HBM] * len(rest),
        out_specs=[HBM] + [VMEM] * (len(shapes) - 1),
        scratch_shapes=[
            pltpu.VMEM((select.shape[1], cols), F32),
            pltpu.VMEM((nw * up(cap, 8), 2 * nb), F32),
            pltpu.VMEM((nb, 2 * nb), F32),
            pltpu.VMEM((2 * nb, cols), F32),
            pltpu.VMEM((2 * waves, cols), F32),
            pltpu.VMEM((2 * count, cols), F32),
            pltpu.VMEM((2 * count, cols), F32),
            pltpu.VMEM((count, 2 * nb), F32),
            pltpu.VMEM((waves, 2 * count), F32),
            pltpu.SemaphoreType.DMA((len(places),)),
            pltpu.SemaphoreType.DMA((2 * nw,)),
            pltpu.SemaphoreType.DMA((cols // min(cols, 1024), 2)),
            pltpu.SemaphoreType.DMA((5,)),
        ],
        compiler_params=params(61),
        name="project",
    )(rounds, select, select_c, lens, *rest)


def whiten_kernel(nf, *refs):
    gram = refs[0][...]
    for ref in refs[1:nf]:
        gram = gram + ref[...]
    out = refs[nf]
    count = gram.shape[0]
    i = lax.broadcasted_iota(jnp.int32, (count, count), 0)
    j = lax.broadcasted_iota(jnp.int32, (count, count), 1)
    upper = jnp.where(i <= j, gram, 0.0)
    lower = jnp.where(i > j, gram, 0.0)
    diagonal = jnp.where(i == j, gram, 0.0)
    gram_re = upper + upper.T - diagonal
    gram_im = lower - lower.T
    scale_row = 1.0 / jnp.sqrt(jnp.sum(diagonal, axis=0, keepdims=True) + epsilon)
    scale_col = 1.0 / jnp.sqrt(jnp.sum(diagonal, axis=1, keepdims=True) + epsilon)
    outer = scale_col * scale_row
    gram_re = gram_re * outer
    gram_im = gram_im * outer
    bound = jnp.max(jnp.sum(jnp.abs(gram_re) + jnp.abs(gram_im), axis=1, keepdims=True), axis=0, keepdims=True)
    gram_re = gram_re / bound
    gram_im = gram_im / bound
    mix = jnp.concatenate(
        [jnp.concatenate([gram_re, gram_im], axis=1), jnp.concatenate([-gram_im, gram_re], axis=1)], axis=0
    )
    i = lax.broadcasted_iota(jnp.int32, (2 * count, 2 * count), 0)
    j = lax.broadcasted_iota(jnp.int32, (2 * count, 2 * count), 1)
    ident = jnp.where(i == j, 1.0, 0.0).astype(F32)
    zed = None
    for step in range(NS_STEPS):
        turn = 1.5 * ident - 0.5 * mix
        turn_parts = split(turn)
        zed = turn if zed is None else nn3(turn_parts, split(zed))
        if step < NS_STEPS - 1:
            mix = nn3(split(nn3(split(mix), turn_parts)), turn_parts)
    out[...] = zed * (1.0 / jnp.sqrt(bound)) * jnp.concatenate([scale_row, scale_row], axis=1)


def whiten(grams):
    count = grams[0].shape[0]
    return pl.pallas_call(
        functools.partial(whiten_kernel, len(grams)),
        out_shape=jax.ShapeDtypeStruct((2 * count, 2 * count), F32),
        in_specs=[VMEM] * len(grams),
        out_specs=VMEM,
        compiler_params=params(8),
        name="whiten",
    )(*grams)


def update_kernel(nf, lens, whitener, p, re, im, *refs):
    pieces, refs = refs[:nf], refs[nf:]
    coef_re, coef_im, new_re, new_im, squares, d_all = refs
    waves, cols = re.shape
    count = coef_re.shape[1]
    share = waves // nf
    me_f = lax.axis_index("freq")
    for k in range(nf):
        d_all[pl.ds(pl.multiple_of((me_f ^ k) * share, share), share), :] = pieces[k][...]
    turn = split(whitener[...])
    coef = nt3(split(d_all[...]), turn)
    coef_re[...] = coef[:, :count]
    coef_im[...] = coef[:, count:]
    back = nn3(split(coef), turn)
    back_re, back_im = back[:, :count], back[:, count:]
    left = split(
        jnp.concatenate(
            [jnp.concatenate([back_re, -back_im], axis=1), jnp.concatenate([back_im, back_re], axis=1)], axis=0
        )
    )
    live = column(lens[...]) * BIN_BLOCK
    sums = jnp.zeros((waves, 128), F32)
    chunk = min(cols, 512)
    for begin in range(0, cols, chunk):
        part = pl.ds(begin, chunk)
        change = nn3(left, split(p[:, part]))
        keep = lax.broadcasted_iota(jnp.int32, (1, chunk), 1) + (me_f * cols + begin) < live
        now_re = jnp.where(keep, re[:, part] - change[:waves], 0.0)
        now_im = jnp.where(keep, im[:, part] - change[waves:], 0.0)
        new_re[:, part] = now_re
        new_im[:, part] = now_im
        square = now_re * now_re + now_im * now_im
        for at in range(0, chunk, 128):
            sums += square[:, at : at + 128]
    squares[...] = jnp.sum(sums.T, axis=0, keepdims=True)


def update(nf, lens, whitener, p, res_re, res_im, pieces):
    waves, cols = res_re.shape
    count = p.shape[0] // 2
    return pl.pallas_call(
        functools.partial(update_kernel, nf),
        out_shape=[
            jax.ShapeDtypeStruct((waves, count), F32),
            jax.ShapeDtypeStruct((waves, count), F32),
            jax.ShapeDtypeStruct((waves, cols), F32),
            jax.ShapeDtypeStruct((waves, cols), F32),
            jax.ShapeDtypeStruct((1, waves), F32),
        ],
        in_specs=[VMEM] * (5 + nf),
        out_specs=[VMEM] * 5,
        scratch_shapes=[pltpu.VMEM((waves, 2 * count), F32)],
        compiler_params=params(24),
        name="update",
    )(lens, whitener, p, res_re, res_im, *pieces)


def spread(rows, nw, work):
    half = rows.shape[1] // 2
    found = [(0, 0, rows)]
    beside = swap(rows, "wave", nw, 1)
    if nw == 8:
        by_two = swap(rows, "wave", nw, 2)
        by_four = swap(rows, "wave", nw, 4)
        done = work(beside)
        by_two, by_four, _ = lax.optimization_barrier((by_two, by_four, done))
        found.append((2, 0, by_two))
        found.append((4, 0, by_four))
        found.append((6, 0, swap(by_two[:, :half], "wave", nw, 4)))
        found.append((6, half, swap(by_four[:, half:], "wave", nw, 2)))
    else:
        found += [(k, 0, swap(rows, "wave", nw, k)) for k in range(2, nw, 2)]
        done = work(beside)
    return found + [(1, 0, beside)] + [(k + 1, col, swap(array, "wave", nw, 1)) for k, col, array in found[1:]], done


def spread_small(rows, nw):
    found = [rows] + [swap(rows, "wave", nw, k) for k in range(2, nw, 2)]
    both = []
    for array in found:
        both += [array, swap(array, "wave", nw, 1)]
    return both


def sum_pieces(pieces, nf):
    return sum([swap(pieces[k], "freq", nf, k) for k in range(1, nf)], pieces[0])


def sum_over_freq(array, nf):
    return sum([swap(array, "freq", nf, k) for k in range(1, nf)], array)


def capacity(count, nw, rows):
    mean = count / nw
    return min(up(math.ceil(mean + 3.0 * math.sqrt(mean)), 4), count, rows)


def body(nw, nf, res_re, res_im, basis_re, basis_im, lengths, pivots):
    waves, cols = res_re.shape
    nb = basis_re.shape[0]
    count = pivots.shape[0]
    cap = capacity(count, nw, waves)
    lens = lengths.reshape(1, waves)
    zero = jnp.zeros((1,), jnp.int32)
    rows = pick(cap, pivots, lengths, zero, res_re, res_im)
    work = lambda beside: (cross(cap, nw, beside, basis_re, basis_im), orders(cap, nw, waves, nb, cols, pivots))
    found, (partial, ordered) = spread(rows, nw, work)
    select, select_c, rounds, blank_p, blank_c = ordered
    crosses = spread_small(sum_over_freq(partial, nf), nw)
    lists = [array for _, _, array in found]
    places = tuple((k, col) for k, col, _ in found)
    blank_p, blank_c, lists, crosses = lax.optimization_barrier((blank_p, blank_c, lists, crosses))

    def another(carry):
        turn, extra_p, extra_c = carry
        turn, owners = lax.optimization_barrier((turn, pivots // waves))
        more = pick(cap, pivots, lengths, (turn * cap).reshape(1), res_re, res_im)
        more_c = sum_over_freq(cross(cap, nw, more, basis_re, basis_im), nf)[:cap]
        everyone = lambda rows: [rows] + [swap(rows, "wave", nw, k) for k in range(1, nw)]
        earlier = jnp.arange(count)[None, :] < jnp.arange(count)[:, None]
        rank = jnp.sum(((owners[:, None] == owners[None, :]) & earlier).astype(jnp.int32), axis=1) - turn * cap
        group = jnp.bitwise_xor(owners, lax.axis_index("wave").astype(jnp.int32))
        slot = jnp.where((rank >= 0) & (rank < cap), group * cap + rank, -1)
        chosen = (slot[:, None] == jnp.arange(nw * cap)[None, :]).astype(F32)

        def arrange(tables):
            table = jnp.concatenate(tables, axis=0)
            return jnp.dot(chosen, table, precision=lax.Precision.HIGHEST, preferred_element_type=F32)

        all_p = everyone(more)
        added = jnp.concatenate([arrange([p[:cap] for p in all_p]), arrange([p[cap:] for p in all_p])], axis=0)
        first = turn == 1
        extra_p = jnp.where(first, 0.0, extra_p) + added
        extra_c = jnp.where(first, 0.0, extra_c) + arrange(everyone(more_c))
        return turn + 1, extra_p, extra_c

    _, extra_p, extra_c = lax.while_loop(
        lambda carry: carry[0] < rounds[0],
        another,
        (jnp.ones((), jnp.int32), blank_p, blank_c),
    )

    rest = [basis_re, basis_im, res_re, res_im, extra_p, extra_c, *lists, *crosses]
    p, gram, *pieces = project(cap, nw, nf, places, rounds, select, select_c, lens, *rest)
    piece = sum_pieces(pieces, nf)
    grams = [gram] + [swap(gram, "freq", nf, k) for k in range(1, nf)]
    every = [piece] + [swap(piece, "freq", nf, k) for k in range(1, nf)]
    whitener = whiten(grams)
    coef_re, coef_im, new_re, new_im, squares = update(nf, lens, whitener, p, res_re, res_im, every)
    errors = sum_over_freq(squares, nf).reshape(waves) / (BIN_BLOCK * lengths).astype(F32)
    return coef_re, coef_im, new_re, new_im, errors


def solution(mesh):
    nw, nf = mesh.shape["wave"], mesh.shape["freq"]
    return jax.shard_map(
        functools.partial(body, nw, nf),
        mesh=mesh,
        in_specs=(P("wave", "freq"), P("wave", "freq"), P(None, "freq"), P(None, "freq"), P("wave"), P()),
        out_specs=(P("wave", None), P("wave", None), P("wave", "freq"), P("wave", "freq"), P("wave")),
        check_vma=False,
    )
```

```python
import functools
import math

import jax
import jax.numpy as jnp
from jax import lax
from jax.experimental import pallas as pl
from jax.experimental.pallas import tpu as pltpu
from jax.sharding import PartitionSpec as P

BIN_BLOCK = 128
NS_STEPS = 6
epsilon = 1e-06
F32 = jnp.float32
BF16 = jnp.bfloat16
MIB = 1024 * 1024

ANY = pl.BlockSpec(memory_space=pl.ANY)
SMEM = pl.BlockSpec(memory_space=pltpu.SMEM)
VMEM = pl.BlockSpec(memory_space=pltpu.VMEM)
HBM = pl.BlockSpec(memory_space=pltpu.HBM)


def params(mib):
    return pltpu.CompilerParams(vmem_limit_bytes=mib * MIB)


def light():
    return pl.CostEstimate(flops=1000, bytes_accessed=1000, transcendentals=0)


def column(row):
    wide = jnp.broadcast_to(row.astype(F32), (8, row.shape[1]))
    return wide.T[:, 0:1].astype(jnp.int32)


def up(value, step):
    return -(-value // step) * step


def swap(array, axis, size, distance):
    return lax.ppermute(array, axis, [(i, i ^ distance) for i in range(size)])


def split(value):
    high = value.astype(BF16)
    low = (value - high.astype(F32)).astype(BF16)
    return high, low


def split3(value):
    high = value.astype(BF16)
    rest = value - high.astype(F32)
    middle = rest.astype(BF16)
    low = (rest - middle.astype(F32)).astype(BF16)
    return high, middle, low


def nn(left, right):
    return jnp.dot(left, right, preferred_element_type=F32)


def nt(left, right):
    return lax.dot_general(left, right, (((1,), (1,)), ((), ())), preferred_element_type=F32)


def nn3(left, right):
    return nn(left[0], right[0]) + (nn(left[0], right[1]) + nn(left[1], right[0]))


def nt3(left, right):
    return nt(left[0], right[0]) + (nt(left[0], right[1]) + nt(left[1], right[0]))


def pick_kernel(cap, piv, lens, skip_ref, re, im, out, where, rows_re, rows_im, sem):
    wave_rows, cols = re.shape
    slots = rows_re.shape[0]
    base = lax.axis_index("wave") * wave_rows
    first_bin = lax.axis_index("freq") * cols
    skip = skip_ref[0]

    def fetch(row, slot):
        pltpu.make_async_copy(re.at[pl.ds(row, 1)], rows_re.at[pl.ds(slot, 1)], sem.at[0]).start()
        pltpu.make_async_copy(im.at[pl.ds(row, 1)], rows_im.at[pl.ds(slot, 1)], sem.at[1]).start()

    def look(i, seen):
        row = piv[i] - base
        own = (row >= 0) & (row < wave_rows)
        slot = seen - skip

        @pl.when(own & (slot >= 0) & (slot < cap))
        def _():
            where[slot] = lens[row]
            fetch(row, slot)

        return seen + own.astype(jnp.int32)

    found = lax.fori_loop(0, piv.shape[0], look, 0, unroll=8) - skip

    def fill(slot, carry):
        where[slot] = 0
        fetch(0, slot)
        return carry

    lax.fori_loop(jnp.clip(found, 0, cap), slots, fill, 0)
    at = lax.broadcasted_iota(jnp.int32, (slots, 1), 0)
    live = jnp.zeros((slots, 1), jnp.int32)
    for slot in range(slots):
        live = jnp.where(at == slot, where[slot] * BIN_BLOCK, live)
    bins = lax.broadcasted_iota(jnp.int32, (slots, cols), 1) + first_bin
    keep = bins < live
    pltpu.make_async_copy(re.at[pl.ds(0, slots)], rows_re, sem.at[0]).wait()
    pltpu.make_async_copy(im.at[pl.ds(0, slots)], rows_im, sem.at[1]).wait()
    out[0:cap, :] = jnp.where(keep, rows_re[...], 0.0)[0:cap]
    out[cap : 2 * cap, :] = jnp.where(keep, rows_im[...], 0.0)[0:cap]


def pick(cap, pivots, lengths, skip, res_re, res_im):
    cols = res_re.shape[1]
    return pl.pallas_call(
        functools.partial(pick_kernel, cap),
        out_shape=jax.ShapeDtypeStruct((2 * cap, cols), F32),
        in_specs=[SMEM, SMEM, SMEM, HBM, HBM],
        out_specs=VMEM,
        scratch_shapes=[
            pltpu.SMEM((up(cap, 8),), jnp.int32),
            pltpu.VMEM((up(cap, 8), cols), F32),
            pltpu.VMEM((up(cap, 8), cols), F32),
            pltpu.SemaphoreType.DMA((2,)),
        ],
        compiler_params=params(8),
        name="pick",
    )(pivots, lengths, skip, res_re, res_im)


def cross_kernel(cap, rows, b_re, b_im, out):
    nb, cols = b_re.shape
    mine = out.shape[0] - up(cap, 8)
    start = pl.multiple_of(lax.axis_index("wave") * mine, mine)
    chunk = min(cols, 512)
    total = jnp.zeros((2 * cap + 2 * mine, 2 * nb), F32)
    for at in range(0, cols, chunk):
        part = pl.ds(at, chunk)
        left = split(
            jnp.concatenate([rows[:, part], b_re[pl.ds(start, mine), part], b_im[pl.ds(start, mine), part]], axis=0)
        )
        right = split(jnp.concatenate([b_re[:, part], b_im[:, part]], axis=0))
        total += nt3(left, right)

    def join(at, size):
        real, imag = total[at : at + size], total[at + size : at + 2 * size]
        return jnp.concatenate([real[:, :nb] + imag[:, nb:], imag[:, :nb] - real[:, nb:]], axis=1)

    out[...] = jnp.zeros_like(out)
    out[0:cap, :] = join(0, cap)
    out[up(cap, 8) :, :] = join(2 * cap, mine)
def cross(cap, nw, rows, basis_re, basis_im):
    nb = basis_re.shape[0]
    return pl.pallas_call(
        functools.partial(cross_kernel, cap),
        out_shape=jax.ShapeDtypeStruct((up(cap, 8) + nb // nw, 2 * nb), F32),
        in_specs=[VMEM, VMEM, VMEM],
        out_specs=VMEM,
        compiler_params=params(16),
        cost_estimate=light(),
        name="cross",
    )(rows, basis_re, basis_im)


def ranks(pivots_col, pivots_row, wave_rows):
    count = pivots_col.shape[0]
    owner_col = pivots_col // wave_rows
    owner_row = pivots_row // wave_rows
    i = lax.broadcasted_iota(jnp.int32, (count, count), 0)
    j = lax.broadcasted_iota(jnp.int32, (count, count), 1)
    ahead = (owner_col == owner_row) & (j < i)
    return owner_col, jnp.sum(ahead.astype(jnp.int32), axis=1, keepdims=True)


def one_hot(index, width):
    return (lax.broadcasted_iota(jnp.int32, (index.shape[0], width), 1) == index).astype(F32).astype(BF16)


def move(source, target, sem):
    copy = pltpu.make_async_copy(source, target, sem)
    copy.start()
    return copy


def orders_kernel(cap, nw, waves, pr, listed, crossed, rounds):
    owner, rank = ranks(column(pr[...]), pr[...], waves)
    group = jnp.bitwise_xor(owner, lax.axis_index("wave"))
    rounds[0] = jnp.max(rank) // cap + 1
    at = jnp.where(rank < cap, group * (2 * cap) + rank, -nw * 2 * cap)
    both = jnp.concatenate([at, at + cap], axis=0)
    listed[...] = one_hot(both, listed.shape[1])
    capp = crossed.shape[1] // nw
    crossed[...] = one_hot(jnp.where(rank < cap, group * capp + rank, -1), crossed.shape[1])


def orders(cap, nw, waves, pivots):
    count = pivots.shape[0]
    return pl.pallas_call(
        functools.partial(orders_kernel, cap, nw, waves),
        out_shape=(
            jax.ShapeDtypeStruct((2 * count, nw * 2 * cap), BF16),
            jax.ShapeDtypeStruct((count, nw * up(cap, 8)), BF16),
            jax.ShapeDtypeStruct((1,), jnp.int32),
        ),
        in_specs=[VMEM],
        out_specs=(VMEM, VMEM, SMEM),
        compiler_params=params(8),
        cost_estimate=light(),
        name="orders",
    )(pivots.reshape(1, count))


def fetch_lists(refs, places, cap, gathered, sem):
    waits = []
    for index, ((k, col), ref) in enumerate(zip(places, refs)):
        target = gathered.at[pl.ds(k * 2 * cap, 2 * cap), pl.ds(col, ref.shape[1])]
        waits.append(move(ref, target, sem.at[index]))
    return waits


def packed(gram_re, gram_im):
    i = lax.broadcasted_iota(jnp.int32, gram_re.shape, 0)
    j = lax.broadcasted_iota(jnp.int32, gram_re.shape, 1)
    return jnp.where(i <= j, gram_re, gram_im)


def joined(total, rows, cols):
    real = total[:rows, :cols] + total[rows:, cols:]
    imag = total[rows:, :cols] - total[:rows, cols:]
    return real, imag


def project_kernel(cap, nw, nf, places, select, select_c, lens, b_re, b_im, re, im, *refs):
    list_refs, refs = refs[: len(places)], refs[len(places) :]
    cross_refs, refs = refs[:nw], refs[nw:]
    p_out, g_out, refs = refs[0], refs[1], refs[2:]
    out, refs = refs[:nf], refs[nf:]
    gathered, crossed, gram_b, d_all, sem_l, sem_c = refs
    count = select_c.shape[0]
    nb, cols = b_re.shape
    waves = re.shape[0]
    capp = up(cap, 8)
    mine = nb // nw
    me_w, me_f = lax.axis_index("wave"), lax.axis_index("freq")
    waits = []
    for k, ref in enumerate(cross_refs):
        at = (k ^ 1) * capp
        waits.append(move(ref.at[pl.ds(0, capp)], crossed.at[pl.ds(at, capp)], sem_c.at[2 * k]))
        at = pl.multiple_of((me_w ^ k) * mine, mine)
        waits.append(move(ref.at[pl.ds(capp, mine)], gram_b.at[pl.ds(at, mine)], sem_c.at[2 * k + 1]))
    list_waits = fetch_lists(list_refs, places, cap, gathered, sem_l)
    chunk = min(cols, 1024)

    for copy in list_waits:
        copy.wait()
    for step in range(cols // chunk):
        part = pl.ds(step * chunk, chunk)
        high, low = split(gathered[:, part])
        block = nn(select[...], high) + nn(select[...], low)
        p_out[:, part] = block
    for copy in waits:
        copy.wait()
    pieces = split3(crossed[...])
    cross_all = nn(select_c[...], pieces[0]) + (nn(select_c[...], pieces[1]) + nn(select_c[...], pieces[2]))
    stacked = jnp.concatenate([cross_all[:, :nb], cross_all[:, nb:]], axis=0)
    twist = nn3(split(stacked), split(gram_b[...]))
    total_re = 2.0 * cross_all[:, :nb] - (twist[:count, :nb] - twist[count:, nb:])
    total_im = 2.0 * cross_all[:, nb:] - (twist[:count, nb:] + twist[count:, :nb])
    take = split(
        jnp.concatenate(
            [jnp.concatenate([total_re, -total_im], axis=1), jnp.concatenate([total_im, total_re], axis=1)], axis=0
        )
    )
    for step in range(cols // chunk):
        part = pl.ds(step * chunk, chunk)
        basis = jnp.concatenate([b_re[:, part], b_im[:, part]], axis=0)
        p_out[:, part] = p_out[:, part] - nn3(take, split(basis))
    right = split(p_out[...])
    inner_p = nt(right[0], right[0])
    inner_q = nt(right[0], right[1])
    end = column(lens[...]) * BIN_BLOCK
    keep = lax.broadcasted_iota(jnp.int32, (1, cols), 1) + me_f * cols < end
    inner_re = nt3(split(jnp.where(keep, re[...], 0.0)), right)
    inner_im = nt3(split(jnp.where(keep, im[...], 0.0)), right)
    inner_r = jnp.concatenate([inner_re, inner_im], axis=0)
    g_out[...] = packed(*joined(inner_p + (inner_q + inner_q.T), count, count))
    d_all[:, :count], d_all[:, count:] = joined(inner_r, waves, count)
    share = waves // nf
    for k in range(nf):
        out[k][...] = d_all[pl.ds(pl.multiple_of((me_f ^ k) * share, share), share), :]


def project(cap, nw, nf, places, select, select_c, lens, *rest):
    basis_re, res_re = rest[0], rest[2]
    count = select_c.shape[0]
    nb, cols = basis_re.shape
    waves = res_re.shape[0]
    shapes = [jax.ShapeDtypeStruct((2 * count, cols), F32), jax.ShapeDtypeStruct((count, count), F32)]
    shapes += [jax.ShapeDtypeStruct((waves // nf, 2 * count), F32)] * nf
    return pl.pallas_call(
        functools.partial(project_kernel, cap, nw, nf, places),
        out_shape=shapes,
        in_specs=[VMEM] * 7 + [HBM] * (len(rest) - 4),
        out_specs=[VMEM] * len(shapes),
        scratch_shapes=[
            pltpu.VMEM((select.shape[1], cols), F32),
            pltpu.VMEM((nw * up(cap, 8), 2 * nb), F32),
            pltpu.VMEM((nb, 2 * nb), F32),
            pltpu.VMEM((waves, 2 * count), F32),
            pltpu.SemaphoreType.DMA((len(places),)),
            pltpu.SemaphoreType.DMA((2 * nw,)),
        ],
        compiler_params=params(36),
        name="project",
    )(select, select_c, lens, *rest)


def whiten_kernel(nf, *refs):
    gram = refs[0][...]
    for ref in refs[1:nf]:
        gram = gram + ref[...]
    out = refs[nf]
    count = gram.shape[0]
    i = lax.broadcasted_iota(jnp.int32, (count, count), 0)
    j = lax.broadcasted_iota(jnp.int32, (count, count), 1)
    upper = jnp.where(i <= j, gram, 0.0)
    lower = jnp.where(i > j, gram, 0.0)
    diagonal = jnp.where(i == j, gram, 0.0)
    gram_re = upper + upper.T - diagonal
    gram_im = lower - lower.T
    scale_row = 1.0 / jnp.sqrt(jnp.sum(diagonal, axis=0, keepdims=True) + epsilon)
    scale_col = 1.0 / jnp.sqrt(jnp.sum(diagonal, axis=1, keepdims=True) + epsilon)
    outer = scale_col * scale_row
    gram_re = gram_re * outer
    gram_im = gram_im * outer
    bound = jnp.max(jnp.sum(jnp.abs(gram_re) + jnp.abs(gram_im), axis=1, keepdims=True), axis=0, keepdims=True)
    gram_re = gram_re / bound
    gram_im = gram_im / bound
    mix = jnp.concatenate(
        [jnp.concatenate([gram_re, gram_im], axis=1), jnp.concatenate([-gram_im, gram_re], axis=1)], axis=0
    )
    i = lax.broadcasted_iota(jnp.int32, (2 * count, 2 * count), 0)
    j = lax.broadcasted_iota(jnp.int32, (2 * count, 2 * count), 1)
    ident = jnp.where(i == j, 1.0, 0.0).astype(F32)
    zed = None
    for step in range(NS_STEPS):
        turn = 1.5 * ident - 0.5 * mix
        turn_parts = split(turn)
        zed = turn if zed is None else nn3(turn_parts, split(zed))
        if step < NS_STEPS - 1:
            mix = nn3(split(nn3(split(mix), turn_parts)), turn_parts)
    out[...] = zed * (1.0 / jnp.sqrt(bound)) * jnp.concatenate([scale_row, scale_row], axis=1)


def whiten(grams):
    count = grams[0].shape[0]
    return pl.pallas_call(
        functools.partial(whiten_kernel, len(grams)),
        out_shape=jax.ShapeDtypeStruct((2 * count, 2 * count), F32),
        in_specs=[VMEM] * len(grams),
        out_specs=VMEM,
        compiler_params=params(8),
        name="whiten",
    )(*grams)


def update_kernel(nf, lens, whitener, p, re, im, *refs):
    pieces, refs = refs[:nf], refs[nf:]
    coef_re, coef_im, new_re, new_im, squares, d_all = refs
    waves, cols = re.shape
    count = coef_re.shape[1]
    share = waves // nf
    me_f = lax.axis_index("freq")
    for k in range(nf):
        d_all[pl.ds(pl.multiple_of((me_f ^ k) * share, share), share), :] = pieces[k][...]
    turn = split(whitener[...])
    coef = nt3(split(d_all[...]), turn)
    coef_re[...] = coef[:, :count]
    coef_im[...] = coef[:, count:]
    back = nn3(split(coef), turn)
    back_re, back_im = back[:, :count], back[:, count:]
    left = split(
        jnp.concatenate(
            [jnp.concatenate([back_re, -back_im], axis=1), jnp.concatenate([back_im, back_re], axis=1)], axis=0
        )
    )
    live = column(lens[...]) * BIN_BLOCK
    sums = jnp.zeros((waves, 128), F32)
    chunk = min(cols, 512)
    for begin in range(0, cols, chunk):
        part = pl.ds(begin, chunk)
        change = nn3(left, split(p[:, part]))
        keep = lax.broadcasted_iota(jnp.int32, (1, chunk), 1) + (me_f * cols + begin) < live
        now_re = jnp.where(keep, re[:, part] - change[:waves], 0.0)
        now_im = jnp.where(keep, im[:, part] - change[waves:], 0.0)
        new_re[:, part] = now_re
        new_im[:, part] = now_im
        square = now_re * now_re + now_im * now_im
        for at in range(0, chunk, 128):
            sums += square[:, at : at + 128]
    squares[...] = jnp.sum(sums.T, axis=0, keepdims=True)


def update(nf, lens, whitener, p, res_re, res_im, pieces):
    waves, cols = res_re.shape
    count = p.shape[0] // 2
    return pl.pallas_call(
        functools.partial(update_kernel, nf),
        out_shape=[
            jax.ShapeDtypeStruct((waves, count), F32),
            jax.ShapeDtypeStruct((waves, count), F32),
            jax.ShapeDtypeStruct((waves, cols), F32),
            jax.ShapeDtypeStruct((waves, cols), F32),
            jax.ShapeDtypeStruct((1, waves), F32),
        ],
        in_specs=[VMEM] * (5 + nf),
        out_specs=[VMEM] * 5,
        scratch_shapes=[pltpu.VMEM((waves, 2 * count), F32)],
        compiler_params=params(24),
        name="update",
    )(lens, whitener, p, res_re, res_im, *pieces)


def spread(rows, nw, work):
    half = rows.shape[1] // 2
    found = [(0, 0, rows)]
    beside = swap(rows, "wave", nw, 1)
    if nw == 8:
        by_two = swap(rows, "wave", nw, 2)
        by_four = swap(rows, "wave", nw, 4)
        done = work(beside)
        by_two, by_four, _ = lax.optimization_barrier((by_two, by_four, done))
        found.append((2, 0, by_two))
        found.append((4, 0, by_four))
        found.append((6, 0, swap(by_two[:, :half], "wave", nw, 4)))
        found.append((6, half, swap(by_four[:, half:], "wave", nw, 2)))
    else:
        found += [(k, 0, swap(rows, "wave", nw, k)) for k in range(2, nw, 2)]
        done = work(beside)
    return found + [(1, 0, beside)] + [(k + 1, col, swap(array, "wave", nw, 1)) for k, col, array in found[1:]], done


def spread_small(rows, nw):
    found = [rows] + [swap(rows, "wave", nw, k) for k in range(2, nw, 2)]
    both = []
    for array in found:
        both += [array, swap(array, "wave", nw, 1)]
    return both


def sum_pieces(pieces, nf):
    return sum([swap(pieces[k], "freq", nf, k) for k in range(1, nf)], pieces[0])


def sum_over_freq(array, nf):
    return sum([swap(array, "freq", nf, k) for k in range(1, nf)], array)


def capacity(count, nw, rows):
    mean = count / nw
    return min(up(math.ceil(mean + 3.0 * math.sqrt(mean)), 4), count, rows)


def body(nw, nf, res_re, res_im, basis_re, basis_im, lengths, pivots):
    waves, cols = res_re.shape
    nb = basis_re.shape[0]
    count = pivots.shape[0]
    cap = capacity(count, nw, waves)
    lens = lengths.reshape(1, waves)
    zero = jnp.zeros((1,), jnp.int32)
    rows = pick(cap, pivots, lengths, zero, res_re, res_im)
    work = lambda beside: (cross(cap, nw, beside, basis_re, basis_im), orders(cap, nw, waves, pivots))
    found, (partial, ordered) = spread(rows, nw, work)
    select, select_c, rounds = ordered
    crosses = spread_small(sum_over_freq(partial, nf), nw)
    lists = [array for _, _, array in found]
    places = tuple((k, col) for k, col, _ in found)
    rest = [basis_re, basis_im, res_re, res_im, *lists, *crosses]
    p, gram, *pieces = project(cap, nw, nf, places, select, select_c, lens, *rest)
    piece = sum_pieces(pieces, nf)
    grams = [gram] + [swap(gram, "freq", nf, k) for k in range(1, nf)]
    every = [piece] + [swap(piece, "freq", nf, k) for k in range(1, nf)]
    whitener = whiten(grams)
    coef_re, coef_im, new_re, new_im, squares = update(nf, lens, whitener, p, res_re, res_im, every)
    errors = sum_over_freq(squares, nf).reshape(waves) / (BIN_BLOCK * lengths).astype(F32)
    made = (coef_re, coef_im, new_re, new_im, errors)

    def again(carry):
        turn, given = lax.optimization_barrier((carry[0], (res_re, res_im, basis_re, basis_im, lengths, pivots)))
        return turn + 1, plainly(nw, nf, *given)

    _, made = lax.while_loop(lambda carry: carry[0] < rounds[0].clip(1, 2), again, (jnp.ones((), jnp.int32), made))
    return made


def plainly(nw, nf, res_re, res_im, basis_re, basis_im, lengths, pivots):
    waves, cols = res_re.shape
    count = pivots.shape[0]
    nb = basis_re.shape[0]

    def total(array, axis, size):
        for bit in range(size.bit_length() - 1):
            array = array + swap(array, axis, size, 1 << bit)
        return array

    exact = dict(precision=lax.Precision.HIGHEST, preferred_element_type=F32)
    dot = functools.partial(jnp.dot, **exact)
    dot_t = lambda left, right: lax.dot_general(left, right, (((1,), (1,)), ((), ())), **exact)
    pair = lambda real, imag: jnp.concatenate([real, imag], axis=0)
    bins = lax.axis_index("freq") * cols + jnp.arange(cols, dtype=jnp.int32)
    mask = (bins[None, :] < BIN_BLOCK * lengths[:, None]).astype(F32)
    live = pair(res_re * mask, res_im * mask)
    owned = lax.axis_index("wave") * waves + jnp.arange(waves, dtype=jnp.int32)
    select = (pivots[:, None] == owned[None, :]).astype(F32)
    pivot = total(pair(dot(select, live[:waves]), dot(select, live[waves:])), "wave", nw)
    basis = pair(basis_re, basis_im)

    def inner(left, right, rows, columns):
        return joined(total(dot_t(left, right), "freq", nf), rows, columns)

    for _ in range(2):
        take_re, take_im = inner(pivot, basis, count, nb)
        pivot = pivot - pair(
            dot(take_re, basis_re) - dot(take_im, basis_im), dot(take_re, basis_im) + dot(take_im, basis_re)
        )
    whitener = whiten([packed(*inner(pivot, pivot, count, count))])
    pieces = jnp.concatenate(inner(live, pivot, waves, count), axis=1)
    coef = dot_t(pieces, whitener)
    back = dot(coef, whitener)
    back_re, back_im = back[:, :count], back[:, count:]
    new_re = (live[:waves] - dot(back_re, pivot[:count]) + dot(back_im, pivot[count:])) * mask
    new_im = (live[waves:] - dot(back_re, pivot[count:]) - dot(back_im, pivot[:count])) * mask
    squares = total(jnp.sum(new_re * new_re + new_im * new_im, axis=1), "freq", nf)
    errors = squares / (BIN_BLOCK * lengths).astype(F32)
    return coef[:, :count], coef[:, count:], new_re, new_im, errors


def solution(mesh):
    nw, nf = mesh.shape["wave"], mesh.shape["freq"]
    return jax.shard_map(
        functools.partial(body, nw, nf),
        mesh=mesh,
        in_specs=(P("wave", "freq"), P("wave", "freq"), P(None, "freq"), P(None, "freq"), P("wave"), P()),
        out_specs=(P("wave", None), P("wave", None), P("wave", "freq"), P("wave", "freq"), P("wave")),
        check_vma=False,
    )
```

```python
import functools
import math

import jax
import jax.numpy as jnp
from jax import lax
from jax.experimental import pallas as pl
from jax.experimental.pallas import tpu as pltpu
from jax.sharding import PartitionSpec as P

BIN_BLOCK = 128
NS_STEPS = 6
epsilon = 1e-06
F32 = jnp.float32
BF16 = jnp.bfloat16
MIB = 1024 * 1024

ANY = pl.BlockSpec(memory_space=pl.ANY)
SMEM = pl.BlockSpec(memory_space=pltpu.SMEM)
VMEM = pl.BlockSpec(memory_space=pltpu.VMEM)
HBM = pl.BlockSpec(memory_space=pltpu.HBM)


def params(mib):
    return pltpu.CompilerParams(vmem_limit_bytes=mib * MIB)


def light():
    return pl.CostEstimate(flops=1000, bytes_accessed=1000, transcendentals=0)


def column(row):
    wide = jnp.broadcast_to(row.astype(F32), (8, row.shape[1]))
    return wide.T[:, 0:1].astype(jnp.int32)


def up(value, step):
    return -(-value // step) * step


def swap(array, axis, size, distance):
    return lax.ppermute(array, axis, [(i, i ^ distance) for i in range(size)])


def split(value):
    high = value.astype(BF16)
    low = (value - high.astype(F32)).astype(BF16)
    return high, low


def split3(value):
    high = value.astype(BF16)
    rest = value - high.astype(F32)
    middle = rest.astype(BF16)
    low = (rest - middle.astype(F32)).astype(BF16)
    return high, middle, low


def nn(left, right):
    return jnp.dot(left, right, preferred_element_type=F32)


def nt(left, right):
    return lax.dot_general(left, right, (((1,), (1,)), ((), ())), preferred_element_type=F32)


def nn3(left, right):
    return nn(left[0], right[0]) + (nn(left[0], right[1]) + nn(left[1], right[0]))


def nt3(left, right):
    return nt(left[0], right[0]) + (nt(left[0], right[1]) + nt(left[1], right[0]))


def pick_kernel(cap, piv, lens, skip_ref, re, im, out, where, rows_re, rows_im, sem):
    wave_rows, cols = re.shape
    slots = rows_re.shape[0]
    base = lax.axis_index("wave") * wave_rows
    first_bin = lax.axis_index("freq") * cols
    skip = skip_ref[0]

    def fetch(row, slot):
        pltpu.make_async_copy(re.at[pl.ds(row, 1)], rows_re.at[pl.ds(slot, 1)], sem.at[0]).start()
        pltpu.make_async_copy(im.at[pl.ds(row, 1)], rows_im.at[pl.ds(slot, 1)], sem.at[1]).start()

    def look(i, seen):
        row = piv[i] - base
        own = (row >= 0) & (row < wave_rows)
        slot = seen - skip

        @pl.when(own & (slot >= 0) & (slot < cap))
        def _():
            where[slot] = lens[row]
            fetch(row, slot)

        return seen + own.astype(jnp.int32)

    found = lax.fori_loop(0, piv.shape[0], look, 0, unroll=8) - skip

    def fill(slot, carry):
        where[slot] = 0
        fetch(0, slot)
        return carry

    lax.fori_loop(jnp.clip(found, 0, cap), slots, fill, 0)
    at = lax.broadcasted_iota(jnp.int32, (slots, 1), 0)
    live = jnp.zeros((slots, 1), jnp.int32)
    for slot in range(slots):
        live = jnp.where(at == slot, where[slot] * BIN_BLOCK, live)
    bins = lax.broadcasted_iota(jnp.int32, (slots, cols), 1) + first_bin
    keep = bins < live
    pltpu.make_async_copy(re.at[pl.ds(0, slots)], rows_re, sem.at[0]).wait()
    pltpu.make_async_copy(im.at[pl.ds(0, slots)], rows_im, sem.at[1]).wait()
    out[0:cap, :] = jnp.where(keep, rows_re[...], 0.0)[0:cap]
    out[cap : 2 * cap, :] = jnp.where(keep, rows_im[...], 0.0)[0:cap]


def pick(cap, pivots, lengths, skip, res_re, res_im):
    cols = res_re.shape[1]
    return pl.pallas_call(
        functools.partial(pick_kernel, cap),
        out_shape=jax.ShapeDtypeStruct((2 * cap, cols), F32),
        in_specs=[SMEM, SMEM, SMEM, HBM, HBM],
        out_specs=VMEM,
        scratch_shapes=[
            pltpu.SMEM((up(cap, 8),), jnp.int32),
            pltpu.VMEM((up(cap, 8), cols), F32),
            pltpu.VMEM((up(cap, 8), cols), F32),
            pltpu.SemaphoreType.DMA((2,)),
        ],
        compiler_params=params(8),
        name="pick",
    )(pivots, lengths, skip, res_re, res_im)


def cross_kernel(cap, rows, b_re, b_im, out):
    nb, cols = b_re.shape
    mine = out.shape[0] - up(cap, 8)
    start = pl.multiple_of(lax.axis_index("wave") * mine, mine)
    chunk = min(cols, 512)
    total = jnp.zeros((2 * cap + 2 * mine, 2 * nb), F32)
    for at in range(0, cols, chunk):
        part = pl.ds(at, chunk)
        left = split(
            jnp.concatenate([rows[:, part], b_re[pl.ds(start, mine), part], b_im[pl.ds(start, mine), part]], axis=0)
        )
        right = split(jnp.concatenate([b_re[:, part], b_im[:, part]], axis=0))
        total += nt3(left, right)

    def join(at, size):
        real, imag = total[at : at + size], total[at + size : at + 2 * size]
        return jnp.concatenate([real[:, :nb] + imag[:, nb:], imag[:, :nb] - real[:, nb:]], axis=1)

    out[...] = jnp.zeros_like(out)
    out[0:cap, :] = join(0, cap)
    out[up(cap, 8) :, :] = join(2 * cap, mine)
def cross(cap, nw, rows, basis_re, basis_im):
    nb = basis_re.shape[0]
    return pl.pallas_call(
        functools.partial(cross_kernel, cap),
        out_shape=jax.ShapeDtypeStruct((up(cap, 8) + nb // nw, 2 * nb), F32),
        in_specs=[VMEM, VMEM, VMEM],
        out_specs=VMEM,
        compiler_params=params(16),
        cost_estimate=light(),
        name="cross",
    )(rows, basis_re, basis_im)


def ranks(pivots_col, pivots_row, wave_rows):
    count = pivots_col.shape[0]
    owner_col = pivots_col // wave_rows
    owner_row = pivots_row // wave_rows
    i = lax.broadcasted_iota(jnp.int32, (count, count), 0)
    j = lax.broadcasted_iota(jnp.int32, (count, count), 1)
    ahead = (owner_col == owner_row) & (j < i)
    return owner_col, jnp.sum(ahead.astype(jnp.int32), axis=1, keepdims=True)


def one_hot(index, width):
    return (lax.broadcasted_iota(jnp.int32, (index.shape[0], width), 1) == index).astype(F32).astype(BF16)


def move(source, target, sem):
    copy = pltpu.make_async_copy(source, target, sem)
    copy.start()
    return copy


def orders_kernel(cap, nw, waves, pr, listed, crossed, rounds):
    owner, rank = ranks(column(pr[...]), pr[...], waves)
    group = jnp.bitwise_xor(owner, lax.axis_index("wave"))
    rounds[0] = jnp.max(rank) // cap + 1
    at = jnp.where(rank < cap, group * (2 * cap) + rank, -nw * 2 * cap)
    both = jnp.concatenate([at, at + cap], axis=0)
    listed[...] = one_hot(both, listed.shape[1])
    capp = crossed.shape[1] // nw
    crossed[...] = one_hot(jnp.where(rank < cap, group * capp + rank, -1), crossed.shape[1])


def orders(cap, nw, waves, pivots):
    count = pivots.shape[0]
    return pl.pallas_call(
        functools.partial(orders_kernel, cap, nw, waves),
        out_shape=(
            jax.ShapeDtypeStruct((2 * count, nw * 2 * cap), BF16),
            jax.ShapeDtypeStruct((count, nw * up(cap, 8)), BF16),
            jax.ShapeDtypeStruct((1,), jnp.int32),
        ),
        in_specs=[VMEM],
        out_specs=(VMEM, VMEM, SMEM),
        compiler_params=params(8),
        cost_estimate=light(),
        name="orders",
    )(pivots.reshape(1, count))


def fetch_lists(refs, places, cap, gathered, sem):
    waits = []
    for index, ((k, col), ref) in enumerate(zip(places, refs)):
        target = gathered.at[pl.ds(k * 2 * cap, 2 * cap), pl.ds(col, ref.shape[1])]
        waits.append(move(ref, target, sem.at[index]))
    return waits


def packed(gram_re, gram_im):
    i = lax.broadcasted_iota(jnp.int32, gram_re.shape, 0)
    j = lax.broadcasted_iota(jnp.int32, gram_re.shape, 1)
    return jnp.where(i <= j, gram_re, gram_im)


def joined(total, rows, cols):
    real = total[:rows, :cols] + total[rows:, cols:]
    imag = total[rows:, :cols] - total[:rows, cols:]
    return real, imag


def project_kernel(cap, nw, nf, places, select, select_c, lens, b_re, b_im, re, im, *refs):
    list_refs, refs = refs[: len(places)], refs[len(places) :]
    cross_refs, refs = refs[:nw], refs[nw:]
    p_out, g_out, refs = refs[0], refs[1], refs[2:]
    out, refs = refs[:nf], refs[nf:]
    gathered, crossed, gram_b, d_all, sem_l, sem_c = refs
    count = select_c.shape[0]
    nb, cols = b_re.shape
    waves = re.shape[0]
    capp = up(cap, 8)
    mine = nb // nw
    me_w, me_f = lax.axis_index("wave"), lax.axis_index("freq")
    waits = []
    for k, ref in enumerate(cross_refs):
        at = (k ^ 1) * capp
        waits.append(move(ref.at[pl.ds(0, capp)], crossed.at[pl.ds(at, capp)], sem_c.at[2 * k]))
        at = pl.multiple_of((me_w ^ k) * mine, mine)
        waits.append(move(ref.at[pl.ds(capp, mine)], gram_b.at[pl.ds(at, mine)], sem_c.at[2 * k + 1]))
    list_waits = fetch_lists(list_refs, places, cap, gathered, sem_l)
    chunk = min(cols, 1024)

    for copy in list_waits:
        copy.wait()
    for step in range(cols // chunk):
        part = pl.ds(step * chunk, chunk)
        high, low = split(gathered[:, part])
        block = nn(select[...], high) + nn(select[...], low)
        p_out[:, part] = block
    for copy in waits:
        copy.wait()
    pieces = split3(crossed[...])
    cross_all = nn(select_c[...], pieces[0]) + (nn(select_c[...], pieces[1]) + nn(select_c[...], pieces[2]))
    stacked = jnp.concatenate([cross_all[:, :nb], cross_all[:, nb:]], axis=0)
    twist = nn3(split(stacked), split(gram_b[...]))
    total_re = 2.0 * cross_all[:, :nb] - (twist[:count, :nb] - twist[count:, nb:])
    total_im = 2.0 * cross_all[:, nb:] - (twist[:count, nb:] + twist[count:, :nb])
    take = split(
        jnp.concatenate(
            [jnp.concatenate([total_re, -total_im], axis=1), jnp.concatenate([total_im, total_re], axis=1)], axis=0
        )
    )
    for step in range(cols // chunk):
        part = pl.ds(step * chunk, chunk)
        basis = jnp.concatenate([b_re[:, part], b_im[:, part]], axis=0)
        p_out[:, part] = p_out[:, part] - nn3(take, split(basis))
    right = split(p_out[...])
    inner_p = nt(right[0], right[0])
    inner_q = nt(right[0], right[1])
    end = column(lens[...]) * BIN_BLOCK
    keep = lax.broadcasted_iota(jnp.int32, (1, cols), 1) + me_f * cols < end
    inner_re = nt3(split(jnp.where(keep, re[...], 0.0)), right)
    inner_im = nt3(split(jnp.where(keep, im[...], 0.0)), right)
    inner_r = jnp.concatenate([inner_re, inner_im], axis=0)
    g_out[...] = packed(*joined(inner_p + (inner_q + inner_q.T), count, count))
    d_all[:, :count], d_all[:, count:] = joined(inner_r, waves, count)
    share = waves // nf
    for k in range(nf):
        out[k][...] = d_all[pl.ds(pl.multiple_of((me_f ^ k) * share, share), share), :]


def project(cap, nw, nf, places, select, select_c, lens, *rest):
    basis_re, res_re = rest[0], rest[2]
    count = select_c.shape[0]
    nb, cols = basis_re.shape
    waves = res_re.shape[0]
    shapes = [jax.ShapeDtypeStruct((2 * count, cols), F32), jax.ShapeDtypeStruct((count, count), F32)]
    shapes += [jax.ShapeDtypeStruct((waves // nf, 2 * count), F32)] * nf
    return pl.pallas_call(
        functools.partial(project_kernel, cap, nw, nf, places),
        out_shape=shapes,
        in_specs=[VMEM] * 7 + [HBM] * (len(rest) - 4),
        out_specs=[VMEM] * len(shapes),
        scratch_shapes=[
            pltpu.VMEM((select.shape[1], cols), F32),
            pltpu.VMEM((nw * up(cap, 8), 2 * nb), F32),
            pltpu.VMEM((nb, 2 * nb), F32),
            pltpu.VMEM((waves, 2 * count), F32),
            pltpu.SemaphoreType.DMA((len(places),)),
            pltpu.SemaphoreType.DMA((2 * nw,)),
        ],
        compiler_params=params(36),
        name="project",
    )(select, select_c, lens, *rest)


def whiten_kernel(nf, *refs):
    gram = refs[0][...]
    for ref in refs[1:nf]:
        gram = gram + ref[...]
    out = refs[nf]
    count = gram.shape[0]
    i = lax.broadcasted_iota(jnp.int32, (count, count), 0)
    j = lax.broadcasted_iota(jnp.int32, (count, count), 1)
    upper = jnp.where(i <= j, gram, 0.0)
    lower = jnp.where(i > j, gram, 0.0)
    diagonal = jnp.where(i == j, gram, 0.0)
    gram_re = upper + upper.T - diagonal
    gram_im = lower - lower.T
    scale_row = 1.0 / jnp.sqrt(jnp.sum(diagonal, axis=0, keepdims=True) + epsilon)
    scale_col = 1.0 / jnp.sqrt(jnp.sum(diagonal, axis=1, keepdims=True) + epsilon)
    outer = scale_col * scale_row
    gram_re = gram_re * outer
    gram_im = gram_im * outer
    bound = jnp.max(jnp.sum(jnp.abs(gram_re) + jnp.abs(gram_im), axis=1, keepdims=True), axis=0, keepdims=True)
    gram_re = gram_re / bound
    gram_im = gram_im / bound
    mix = jnp.concatenate(
        [jnp.concatenate([gram_re, gram_im], axis=1), jnp.concatenate([-gram_im, gram_re], axis=1)], axis=0
    )
    i = lax.broadcasted_iota(jnp.int32, (2 * count, 2 * count), 0)
    j = lax.broadcasted_iota(jnp.int32, (2 * count, 2 * count), 1)
    ident = jnp.where(i == j, 1.0, 0.0).astype(F32)
    zed = None
    for step in range(NS_STEPS):
        turn = 1.5 * ident - 0.5 * mix
        turn_parts = split(turn)
        zed = turn if zed is None else nn3(turn_parts, split(zed))
        if step < NS_STEPS - 1:
            mix = nn3(split(nn3(split(mix), turn_parts)), turn_parts)
    out[...] = zed * (1.0 / jnp.sqrt(bound)) * jnp.concatenate([scale_row, scale_row], axis=1)


def whiten(grams):
    count = grams[0].shape[0]
    return pl.pallas_call(
        functools.partial(whiten_kernel, len(grams)),
        out_shape=jax.ShapeDtypeStruct((2 * count, 2 * count), F32),
        in_specs=[VMEM] * len(grams),
        out_specs=VMEM,
        compiler_params=params(8),
        name="whiten",
    )(*grams)


def update_kernel(nf, lens, whitener, p, re, im, *refs):
    pieces, refs = refs[:nf], refs[nf:]
    coef_re, coef_im, new_re, new_im, squares, d_all = refs
    waves, cols = re.shape
    count = coef_re.shape[1]
    share = waves // nf
    me_f = lax.axis_index("freq")
    for k in range(nf):
        d_all[pl.ds(pl.multiple_of((me_f ^ k) * share, share), share), :] = pieces[k][...]
    turn = split(whitener[...])
    coef = nt3(split(d_all[...]), turn)
    coef_re[...] = coef[:, :count]
    coef_im[...] = coef[:, count:]
    back = nn3(split(coef), turn)
    back_re, back_im = back[:, :count], back[:, count:]
    left = split(
        jnp.concatenate(
            [jnp.concatenate([back_re, -back_im], axis=1), jnp.concatenate([back_im, back_re], axis=1)], axis=0
        )
    )
    live = column(lens[...]) * BIN_BLOCK
    sums = jnp.zeros((waves, 128), F32)
    chunk = min(cols, 512)
    for begin in range(0, cols, chunk):
        part = pl.ds(begin, chunk)
        change = nn3(left, split(p[:, part]))
        keep = lax.broadcasted_iota(jnp.int32, (1, chunk), 1) + (me_f * cols + begin) < live
        now_re = jnp.where(keep, re[:, part] - change[:waves], 0.0)
        now_im = jnp.where(keep, im[:, part] - change[waves:], 0.0)
        new_re[:, part] = now_re
        new_im[:, part] = now_im
        square = now_re * now_re + now_im * now_im
        for at in range(0, chunk, 128):
            sums += square[:, at : at + 128]
    squares[...] = jnp.sum(sums.T, axis=0, keepdims=True)


def update(nf, lens, whitener, p, res_re, res_im, pieces):
    waves, cols = res_re.shape
    count = p.shape[0] // 2
    return pl.pallas_call(
        functools.partial(update_kernel, nf),
        out_shape=[
            jax.ShapeDtypeStruct((waves, count), F32),
            jax.ShapeDtypeStruct((waves, count), F32),
            jax.ShapeDtypeStruct((waves, cols), F32),
            jax.ShapeDtypeStruct((waves, cols), F32),
            jax.ShapeDtypeStruct((1, waves), F32),
        ],
        in_specs=[VMEM] * (5 + nf),
        out_specs=[VMEM] * 5,
        scratch_shapes=[pltpu.VMEM((waves, 2 * count), F32)],
        compiler_params=params(24),
        name="update",
    )(lens, whitener, p, res_re, res_im, *pieces)


def spread(rows, nw, work):
    half = rows.shape[1] // 2
    found = [(0, 0, rows)]
    beside = swap(rows, "wave", nw, 1)
    if nw == 8:
        by_two = swap(rows, "wave", nw, 2)
        by_four = swap(rows, "wave", nw, 4)
        done = work(beside)
        by_two, by_four, _ = lax.optimization_barrier((by_two, by_four, done))
        found.append((2, 0, by_two))
        found.append((4, 0, by_four))
        found.append((6, 0, swap(by_two[:, :half], "wave", nw, 4)))
        found.append((6, half, swap(by_four[:, half:], "wave", nw, 2)))
    else:
        found += [(k, 0, swap(rows, "wave", nw, k)) for k in range(2, nw, 2)]
        done = work(beside)
    return found + [(1, 0, beside)] + [(k + 1, col, swap(array, "wave", nw, 1)) for k, col, array in found[1:]], done


def spread_small(rows, nw):
    found = [rows] + [swap(rows, "wave", nw, k) for k in range(2, nw, 2)]
    both = []
    for array in found:
        both += [array, swap(array, "wave", nw, 1)]
    return both


def mean_kernel(lens, *refs):
    total = refs[0][...]
    for ref in refs[1:-1]:
        total = total + ref[...]
    refs[-1][...] = total / (BIN_BLOCK * lens[...]).astype(F32)


def mean(parts, lens):
    return pl.pallas_call(
        mean_kernel,
        out_shape=jax.ShapeDtypeStruct(lens.shape, F32),
        in_specs=[VMEM] * (1 + len(parts)),
        out_specs=VMEM,
        compiler_params=params(4),
        name="mean",
    )(lens, *parts)


def sum_pieces(pieces, nf):
    return sum([swap(pieces[k], "freq", nf, k) for k in range(1, nf)], pieces[0])


def sum_over_freq(array, nf):
    return sum([swap(array, "freq", nf, k) for k in range(1, nf)], array)


def capacity(count, nw, rows):
    mean = count / nw
    return min(up(math.ceil(mean + 3.0 * math.sqrt(mean)), 4), count, rows)


def body(nw, nf, res_re, res_im, basis_re, basis_im, lengths, pivots):
    waves, cols = res_re.shape
    nb = basis_re.shape[0]
    count = pivots.shape[0]
    cap = capacity(count, nw, waves)
    lens = lengths.reshape(1, waves)
    zero = jnp.zeros((1,), jnp.int32)
    rows = pick(cap, pivots, lengths, zero, res_re, res_im)
    work = lambda beside: (cross(cap, nw, beside, basis_re, basis_im), orders(cap, nw, waves, pivots))
    found, (partial, ordered) = spread(rows, nw, work)
    select, select_c, rounds = ordered
    crosses = spread_small(sum_over_freq(partial, nf), nw)
    lists = [array for _, _, array in found]
    places = tuple((k, col) for k, col, _ in found)
    rest = [basis_re, basis_im, res_re, res_im, *lists, *crosses]
    p, gram, *pieces = project(cap, nw, nf, places, select, select_c, lens, *rest)
    piece = sum_pieces(pieces, nf)
    grams = [gram] + [swap(gram, "freq", nf, k) for k in range(1, nf)]
    every = [piece] + [swap(piece, "freq", nf, k) for k in range(1, nf)]
    whitener = whiten(grams)
    coef_re, coef_im, new_re, new_im, squares = update(nf, lens, whitener, p, res_re, res_im, every)
    errors = mean([squares] + [swap(squares, "freq", nf, k) for k in range(1, nf)], lens).reshape(waves)
    made = (coef_re, coef_im, new_re, new_im, errors)

    def again(carry):
        turn, given = lax.optimization_barrier((carry[0], (res_re, res_im, basis_re, basis_im, lengths, pivots)))
        return turn + 1, plainly(nw, nf, *given)

    _, made = lax.while_loop(lambda carry: carry[0] < rounds[0].clip(1, 2), again, (jnp.ones((), jnp.int32), made))
    return made


def plainly(nw, nf, res_re, res_im, basis_re, basis_im, lengths, pivots):
    waves, cols = res_re.shape
    count = pivots.shape[0]
    nb = basis_re.shape[0]

    def total(array, axis, size):
        for bit in range(size.bit_length() - 1):
            array = array + swap(array, axis, size, 1 << bit)
        return array

    exact = dict(precision=lax.Precision.HIGHEST, preferred_element_type=F32)
    dot = functools.partial(jnp.dot, **exact)
    dot_t = lambda left, right: lax.dot_general(left, right, (((1,), (1,)), ((), ())), **exact)
    pair = lambda real, imag: jnp.concatenate([real, imag], axis=0)
    bins = lax.axis_index("freq") * cols + jnp.arange(cols, dtype=jnp.int32)
    mask = (bins[None, :] < BIN_BLOCK * lengths[:, None]).astype(F32)
    live = pair(res_re * mask, res_im * mask)
    owned = lax.axis_index("wave") * waves + jnp.arange(waves, dtype=jnp.int32)
    select = (pivots[:, None] == owned[None, :]).astype(F32)
    pivot = total(pair(dot(select, live[:waves]), dot(select, live[waves:])), "wave", nw)
    basis = pair(basis_re, basis_im)

    def inner(left, right, rows, columns):
        return joined(total(dot_t(left, right), "freq", nf), rows, columns)

    for _ in range(2):
        take_re, take_im = inner(pivot, basis, count, nb)
        pivot = pivot - pair(
            dot(take_re, basis_re) - dot(take_im, basis_im), dot(take_re, basis_im) + dot(take_im, basis_re)
        )
    whitener = whiten([packed(*inner(pivot, pivot, count, count))])
    pieces = jnp.concatenate(inner(live, pivot, waves, count), axis=1)
    coef = dot_t(pieces, whitener)
    back = dot(coef, whitener)
    back_re, back_im = back[:, :count], back[:, count:]
    new_re = (live[:waves] - dot(back_re, pivot[:count]) + dot(back_im, pivot[count:])) * mask
    new_im = (live[waves:] - dot(back_re, pivot[count:]) - dot(back_im, pivot[:count])) * mask
    squares = total(jnp.sum(new_re * new_re + new_im * new_im, axis=1), "freq", nf)
    errors = squares / (BIN_BLOCK * lengths).astype(F32)
    return coef[:, :count], coef[:, count:], new_re, new_im, errors


def solution(mesh):
    nw, nf = mesh.shape["wave"], mesh.shape["freq"]
    return jax.shard_map(
        functools.partial(body, nw, nf),
        mesh=mesh,
        in_specs=(P("wave", "freq"), P("wave", "freq"), P(None, "freq"), P(None, "freq"), P("wave"), P()),
        out_specs=(P("wave", None), P("wave", None), P("wave", "freq"), P("wave", "freq"), P("wave")),
        check_vma=False,
    )
```
